128 devices in a mesh: var: 4 (over z), samp: 32 (over x, y, core).
Axes of the slice: x: 4, y: 4, z: 4, core: 2. Of those that a mesh axis runs over, the one named last changes fastest.
Arguments:
- genotypes: int32 [3072, 98304], P('var', 'samp'), may hold values from 0 to 2, as said below
- called: int32 [3072, 98304], P('var', 'samp'), may hold values from 0 to 1
- dosage: int32 [98304, 1024], P(('samp', 'var')), may hold values from 0 to 200
- sample_order: int32 [128, 768], P(('samp', 'var')), may hold values from 0 to 767, each once within a row
- noise_ratio: float32 [16], replicated, may hold values from 0.5 to 4
- solution: float32 [98304, 16], P(('samp', 'var')), may hold values from -13 to 13
- residual: float32 [98304, 16], P(('samp', 'var')), may hold values from -13 to 13
- direction: float32 [98304, 16], P(('samp', 'var')), may hold values from -13 to 13
Outputs:
- solution_new: float32 [98304, 16], P(('samp', 'var'))
- residual_new: float32 [98304, 16], P(('samp', 'var'))
- direction_new: float32 [98304, 16], P(('samp', 'var'))
- scores: float32 [1024, 16], P(('var', 'samp'))
The draws below stay inside these ranges and needn't reach their ends.
Inputs may be any that keep to these rules, and one draw needn't show every extreme that they name: `genotypes`: where called is 1, the count of one allele. `sample_order`: each row lists 0 to 767 once.
All inputs are finite; a program needn't handle non-finite values.
Results may differ from the reference program's by a relative error of at most 0.023.
Values may be sent and summed in bfloat16 or wider, within the bound.
A program may use at most 128 MiB of HBM per device.

```python
import math
import jax
import jax.numpy as jnp
from jax import lax

VARIANTS = 3072
IMPUTED = 1024
RHS = 16
SAMPLES = 98304
QUARTER = 768
BLOCKS = 128


def allele_pair(key, limit):
    key_first, key_second = jax.random.split(key, 2)
    first = jnp.where(jax.random.randint(key_first, (VARIANTS, SAMPLES), 0, 1000) < limit, 1, 0)
    second = jnp.where(jax.random.randint(key_second, (VARIANTS, SAMPLES), 0, 1000) < limit, 1, 0)
    return (first + second).astype(jnp.int32)


def trend_place(key):
    sample = jnp.arange(SAMPLES, dtype=jnp.int32)[None, :]
    flipped = jax.random.randint(key, (VARIANTS, 1), 0, 2)
    return jnp.where(flipped == 1, SAMPLES - 1 - sample, sample)


def draw_genotypes(key, part):
    key_base, key_codes, key_sign = jax.random.split(jax.random.fold_in(key, 17), 3)
    base = jax.random.randint(key_base, (VARIANTS, 1), 40, 241)
    place = trend_place(key_sign)
    limit = base * (SAMPLES + 3 * place) // SAMPLES
    return allele_pair(key_codes, limit)


def draw_called(key, part):
    key_mask, key_sign = jax.random.split(jax.random.fold_in(key, 29), 2)
    place = trend_place(key_sign)
    limit = 300 + 600 * place // SAMPLES
    drawn = jax.random.randint(key_mask, (VARIANTS, SAMPLES), 0, 1000)
    return jnp.where(drawn < limit, 1, 0).astype(jnp.int32)


def draw_dosage(key, part):
    key_ceiling, key_value = jax.random.split(jax.random.fold_in(key, 41), 2)
    ceiling = jax.random.randint(key_ceiling, (1, IMPUTED), 50, 68)
    sample = jnp.arange(SAMPLES, dtype=jnp.int32)[:, None]
    top = jnp.minimum(ceiling * (SAMPLES + 3 * sample) // SAMPLES, 200)
    return jax.random.randint(key_value, (SAMPLES, IMPUTED), 0, top + 1).astype(jnp.int32)


def vector_draw(key, salt):
    key_row, key_col, key_noise = jax.random.split(jax.random.fold_in(key, salt), 3)
    rows = jnp.arange(SAMPLES, dtype=jnp.float32)[:, None] / SAMPLES
    row_scale = jnp.exp(jax.random.uniform(key_row, (SAMPLES, 1), minval=0.0, maxval=math.log(10.0)))
    col_scale = jnp.exp(jax.random.uniform(key_col, (1, RHS), minval=0.0, maxval=math.log(10.0)))
    values = jnp.clip(jax.random.normal(key_noise, (SAMPLES, RHS)), -4.0, 4.0)
    rise = jnp.sqrt(1.0 + 2.0 * rows)
    return jnp.clip(0.1 * values * row_scale * col_scale * rise, -12.5, 12.5).astype(jnp.float32)


def draw_solution(key, part):
    return vector_draw(key, 101)


def draw_residual(key, part):
    return vector_draw(key, 202)


def draw_direction(key, part):
    return vector_draw(key, 303)


def setup_inputs(seed: int = 0) -> dict:
    arg_keys = jax.random.split(jax.random.key(seed), 9)
    return {
        "genotypes": draw_genotypes(jax.random.fold_in(arg_keys[8], 71), 0),
        "called": draw_called(jax.random.fold_in(arg_keys[8], 71), 0),
        "dosage": draw_dosage(jax.random.fold_in(arg_keys[8], 71), 0),
        "sample_order": jax.vmap(lambda own: jax.random.permutation(own, QUARTER))(jax.random.split(arg_keys[3], BLOCKS)).reshape((BLOCKS, QUARTER)).astype(jnp.int32),
        "noise_ratio": jnp.clip(jnp.exp(jax.random.uniform(arg_keys[4], (RHS,), jnp.float32, math.log(0.5), math.log(4.0))), 0.5, 4.0),
        "solution": draw_solution(jax.random.fold_in(arg_keys[8], 71), 0),
        "residual": draw_residual(jax.random.fold_in(arg_keys[8], 71), 0),
        "direction": draw_direction(jax.random.fold_in(arg_keys[8], 71), 0),
    }


def widen(values):
    return lax.optimization_barrier(values.astype(jnp.bfloat16)).astype(jnp.float32)

def product(matrix, vectors):
    return jnp.dot(matrix, vectors, preferred_element_type=jnp.float32, precision=lax.Precision.HIGHEST)

def reference(genotypes, called, dosage, sample_order, noise_ratio, solution, residual, direction):
    pieces = 4
    block_width = VARIANTS // pieces
    direction_b = widen(direction)
    frequencies = []
    spreads = []
    loadings = []
    for position in range(pieces):
        first_row = position * block_width
        codes_block = genotypes[first_row:first_row + block_width]
        called_block = called[first_row:first_row + block_width]
        coded = codes_block * called_block
        called_count = lax.optimization_barrier(jnp.sum(called_block, axis=1)).astype(jnp.float32)
        allele_sum = lax.optimization_barrier(jnp.sum(coded, axis=1)).astype(jnp.float32)
        frequency = (allele_sum + 1.0) / (2.0 * called_count + 2.0)
        spread = jnp.sqrt(2.0 * frequency * (1.0 - frequency))
        raw_proj = product(coded.astype(jnp.float32), direction_b)
        called_proj = product(called_block.astype(jnp.float32), direction_b)
        loading = (raw_proj - 2.0 * frequency[:, None] * called_proj) / spread[:, None]
        frequencies.append(frequency)
        spreads.append(spread)
        loadings.append(loading)
    back = jnp.zeros(direction.shape, jnp.float32)
    for position in range(pieces):
        first_row = position * block_width
        codes_block = genotypes[first_row:first_row + block_width]
        called_block = called[first_row:first_row + block_width]
        coded = (codes_block * called_block).astype(jnp.float32)
        scaled_a = widen(loadings[position] / spreads[position][:, None])
        scaled_b = widen(2.0 * frequencies[position][:, None] * loadings[position] / spreads[position][:, None])
        back = back + product(coded.T, scaled_a) - product(called_block.astype(jnp.float32).T, scaled_b)
    applied = noise_ratio[None, :] * direction + back / VARIANTS
    res_norm = lax.optimization_barrier(jnp.sum(residual * residual, axis=0))
    curvature = lax.optimization_barrier(jnp.sum(direction * applied, axis=0))
    step_size = res_norm / (curvature + 1e-06)
    solution_new = solution + step_size[None, :] * direction
    residual_new = residual - step_size[None, :] * applied
    res_new_norm = lax.optimization_barrier(jnp.sum(residual_new * residual_new, axis=0))
    direction_new = residual_new + (res_new_norm / (res_norm + 1e-06))[None, :] * direction
    rows = (jnp.arange(BLOCKS, dtype=jnp.int32)[:, None] * QUARTER + sample_order.astype(jnp.int32)).reshape(-1)
    picked = widen(jnp.take(solution_new, rows, axis=0))
    dosage_sum = lax.optimization_barrier(jnp.sum(dosage, axis=0)).astype(jnp.float32)
    cross_sum = product(dosage.astype(jnp.float32).T, picked)
    sol_sum = lax.optimization_barrier(jnp.sum(solution_new, axis=0))
    sol_square = lax.optimization_barrier(jnp.sum(solution_new * solution_new, axis=0))
    dose_freq = (dosage_sum / 100.0 + 1.0) / (2.0 * SAMPLES + 2.0)
    dose_spread = jnp.sqrt(2.0 * dose_freq * (1.0 - dose_freq))
    scale_norm = math.sqrt(SAMPLES) * jnp.sqrt(sol_square / SAMPLES + 1e-06)
    scores = (cross_sum / 100.0 - 2.0 * dose_freq[:, None] * sol_sum[None, :]) / (dose_spread[:, None] * scale_norm[None, :])
    return (solution_new, residual_new, direction_new, scores)
```

```python
import functools
import math

import jax
import jax.numpy as jnp
from jax import lax
from jax.experimental import pallas as pl
from jax.experimental.pallas import tpu as pltpu
from jax.sharding import PartitionSpec as P

VARIANTS = 3072
SAMPLES = 98304
IMPUTED = 1024
RHS = 16
NZ = 4
NP = 32
QUARTER = 768
WIDE = QUARTER * NZ
LOCAL = VARIANTS // NZ
BLK = 128
NBLK = LOCAL // BLK
F32 = jnp.float32
BF16 = jnp.bfloat16
MESH = pl.DeviceIdType.MESH


def owner_of(block, group):
    far = block + 10 - 4 * lax.rem(block // 2, 2)
    return 2 * (block + group * (far - block)) + group


def rows_iota(shape):
    return lax.broadcasted_iota(jnp.int32, shape, 0)


def lanes_iota(shape):
    return lax.broadcasted_iota(jnp.int32, shape, 1)


def to_column(row):
    eye = rows_iota((RHS, RHS)) == lanes_iota((RHS, RHS))
    return jnp.sum(jnp.where(eye, jnp.broadcast_to(row, (RHS, RHS)), 0.0), axis=1, keepdims=True)


def spread_columns(columns):
    rows, lanes = rows_iota((RHS, 128)), lanes_iota((RHS, 128))
    total = jnp.zeros((RHS, 128), F32)
    for k, column in enumerate(columns):
        total = jnp.where(lanes == rows + RHS * k, column, total)
    return total[:8] + total[8:]


def kernel(
    gen, cal, dos, order, noise, sol, res, dirn,
    sol_new, res_new, dir_new, scores,
    gv, cv, dv, xb, dx, db, hot, stat_s, stat_r, rs_s, rs_r, ag_s, ag_r, g_acc, g_s, g_r,
    q_acc, q_r, cz_s, cz_r, cp_s, cp_r, d1_s, d1_r, d2_s, d2_r,
    load_sem, a_send, a_recv, st_send, st_recv, rs_send, rs_recv, ag_send, ag_recv,
    g_send, g_recv, q_send, q_recv, cz_send, cz_recv, cp_send, cp_recv, d1_send, d1_recv, d2_send, d2_recv,
):
    z = lax.axis_index("var")
    me = lax.axis_index("samp")
    core = lax.rem(me, 2)
    chip = me // 2

    def z_peer(k):
        return {"var": lax.rem(z + k, NZ), "samp": me}

    def p_peer(k):
        return {"var": z, "samp": lax.rem(me + k, NP)}

    def d1_peer(k):
        return {"var": lax.rem(z + k // 2, NZ), "samp": 2 * chip + lax.rem(core + lax.rem(k, 2), 2)}

    def remote(src, dst, send, recv, device):
        return pltpu.make_async_remote_copy(
            src_ref=src, dst_ref=dst, send_sem=send, recv_sem=recv, device_id=device, device_id_type=MESH
        )

    def load(j, which):
        source, target = ((gen, gv), (cal, cv))[which]
        return pltpu.make_async_copy(
            source.at[pl.ds(pl.multiple_of(j * BLK, BLK), BLK), :], target.at[j], load_sem.at[which, j]
        )

    load_dos = pltpu.make_async_copy(dos, dv, load_sem.at[0, NBLK])

    for j in range(3):
        load(j, 0).start()
        load(j, 1).start()

    barrier = pltpu.get_barrier_semaphore()

    def greet_plane(k, carry):
        pl.semaphore_signal(barrier, inc=1, device_id=p_peer(k), device_id_type=MESH)
        return carry

    def greet_near(k, carry):
        pl.semaphore_signal(barrier, inc=1, device_id=d1_peer(k), device_id_type=MESH)
        return carry

    lax.fori_loop(1, NP, greet_plane, 0)
    lax.fori_loop(2, 8, greet_near, 0)

    d = dirn[...]
    r = res[...]
    d_b = d.astype(BF16)
    dx[:RHS, pl.ds(pl.multiple_of(z * QUARTER, QUARTER), QUARTER)] = d_b
    dx[RHS:, :] = jnp.ones((RHS, WIDE), BF16)
    r_col = jnp.sum(r * r, axis=1, keepdims=True)
    d_col = jnp.sum(d * d, axis=1, keepdims=True)
    pair = jnp.sum(spread_columns((r_col, d_col)), axis=0, keepdims=True)
    row8, lane8 = rows_iota((8, 128)), lanes_iota((8, 128))
    stat_s[...] = jnp.where(row8 == 2, pair, jnp.where(row8 == 3, pltpu.roll(jnp.broadcast_to(pair, (8, 128)), 112, 1), 0.0))
    g_acc[...] = jnp.zeros((RHS, WIDE), F32)
    q_acc[...] = jnp.zeros((8, 128), F32)

    pl.semaphore_wait(barrier, NP - 1 + 6)

    def direction_copy(k):
        mine = dx.at[pl.ds(0, RHS), pl.ds(pl.multiple_of(z * QUARTER, QUARTER), QUARTER)]
        return remote(mine, mine, a_send.at[k - 1], a_recv.at[k - 1], z_peer(k))

    def stat_copy(k):
        return remote(stat_s, stat_r.at[k - 1], st_send.at[k - 1], st_recv.at[k - 1], z_peer(k))

    for k in range(1, NZ):
        direction_copy(k).start()
        stat_copy(k).start()
    for k in range(1, NZ):
        stat_copy(k).wait()
    stats = stat_s[...] + stat_r[0] + stat_r[1] + stat_r[2]
    for k in range(1, NZ):
        direction_copy(k).wait()

    def rs_copy(j, group):
        owner = owner_of(j, group)
        slot = lax.rem(me - owner + NP - 1 + NP, NP)
        return remote(
            rs_s.at[j, group], rs_r.at[slot], rs_send.at[j, group], rs_recv, {"var": z, "samp": owner}
        )

    def chunk(j):
        load(j, 0).wait()
        load(j, 1).wait()

        @pl.when(j + 3 < NBLK)
        def _():
            load(j + 3, 0).start()
            load(j + 3, 1).start()

        @pl.when(j + 3 == NBLK)
        def _():
            load_dos.start()

        def convert(i, carry):
            first = pl.multiple_of(i * 16, 16)
            called = cv[j, pl.ds(first, 16), :].astype(F32).astype(BF16)
            codes = gv[j, pl.ds(first, 16), :].astype(F32).astype(BF16)
            xb[j, pl.ds(first, 16), :] = codes * called
            xb[j, pl.ds(pl.multiple_of(first + BLK, 16), 16), :] = called
            return carry

        lax.fori_loop(0, BLK // 16, convert, 0)
        proj = lax.dot_general(dx[...], xb[j], (((1,), (1,)), ((), ())), preferred_element_type=F32)
        counts = jnp.where(row8 == 0, proj[16:24, :BLK], jnp.where(row8 == 1, proj[16:24, BLK:], stats))
        for group in range(2):
            rs_s[j, group, 0:8, :] = proj[8 * group:8 * group + 8, :BLK]
            rs_s[j, group, 8:16, :] = proj[8 * group:8 * group + 8, BLK:]
            rs_s[j, group, 16:24, :] = counts

            @pl.when(me != owner_of(j, group))
            def _():
                rs_copy(j, group).start()

    def ag_copy(j, group, k):
        return remote(ag_r.at[j, group], ag_r.at[j, group], ag_send, ag_recv.at[j, group], p_peer(k))

    def owner_part(j):
        first, second = owner_of(j, 0), owner_of(j, 1)

        @pl.when((me == first) | (me == second))
        def _():
            group = (me == second).astype(jnp.int32)
            pltpu.make_async_copy(rs_r, rs_r, rs_recv).wait()
            total = rs_s[j, group] + jnp.sum(rs_r[...], axis=0)
            raw, called = total[0:8], total[8:16]
            frequency = (total[16:17] + 1.0) / (2.0 * total[17:18] + 2.0)
            spread = jnp.sqrt(2.0 * frequency * (1.0 - frequency))
            loading = (raw - 2.0 * frequency * called) / spread
            scaled_a = loading / spread
            scaled_b = 2.0 * frequency * loading / spread
            square = jnp.sum(loading * loading, axis=1, keepdims=True)
            square = jnp.sum(jnp.where(lane8 == row8 + 8 * group, square, 0.0), axis=0, keepdims=True)
            tail = jnp.where(row8 == 0, square, jnp.where((row8 == 2) | (row8 == 3), total[16:24], 0.0))
            high = tail.astype(BF16).astype(F32)
            ag_r[j, group] = jnp.concatenate([scaled_a, -scaled_b, high, tail - high], axis=0).astype(BF16)

            def send(k, carry):
                ag_copy(j, group, k).start()
                return carry

            lax.fori_loop(1, NP, send, 0)

    def back(j):
        halves = []
        for group in range(2):
            @pl.when(me != owner_of(j, group))
            def _():
                ag_copy(j, group, 1).wait_recv()

            halves.append(ag_r[j, group].astype(F32))
        left = jnp.concatenate([half[0:8] for half in halves], axis=0)
        right = jnp.concatenate([half[8:16] for half in halves], axis=0)
        weights = jnp.concatenate([left, right], axis=1).astype(BF16)
        q_acc[...] += (halves[0][16:24] + halves[0][24:32]) + (halves[1][16:24] + halves[1][24:32])
        return weights

    def back_product(j, weights):
        g_acc[...] += jnp.dot(weights, xb[j], preferred_element_type=F32)

    def step(j, carry):
        chunk(j)

        @pl.when(j >= 2)
        def _():
            owner_part(j - 2)

        @pl.when(j >= 4)
        def _():
            back_product(j - 4, back(j - 4))

        return carry

    lax.fori_loop(0, NBLK, step, 0)
    owner_part(NBLK - 2)

    load_dos.wait()

    def one_hot(i, carry):
        first = pl.multiple_of(i * 16, 16)
        hot[pl.ds(first, 16), :] = jnp.where(rows_iota((16, QUARTER)) + first == order[...], 1.0, 0.0).astype(BF16)
        return carry

    lax.fori_loop(0, QUARTER // 16, one_hot, 0)

    def convert_dose(i, carry):
        first = pl.multiple_of(i * 16, 16)
        db[pl.ds(first, 16), :] = dv[pl.ds(first, 16), :].astype(F32).astype(BF16)
        return carry

    lax.fori_loop(0, QUARTER // 16, convert_dose, 0)
    s = sol[...]
    s_high = s.astype(BF16)
    s_low = (s - s_high.astype(F32)).astype(BF16)
    d_low = (d - d_b.astype(F32)).astype(BF16)
    parts = jnp.concatenate([s_high, s_low, d_b, d_low], axis=0)
    picked = jnp.dot(parts, hot[...], preferred_element_type=F32).astype(BF16)
    picked = jnp.concatenate([picked, jnp.ones((RHS, QUARTER), BF16)], axis=0)
    cross = jnp.dot(picked, db[...], preferred_element_type=F32)
    cz_s[0:16, :] = cross[0:16] + cross[16:32]
    cz_s[16:32, :] = cross[32:48] + cross[48:64]
    cz_s[32:40, :] = cross[64:72]
    part = IMPUTED // NZ

    def cz_copy(k):
        peer = lax.rem(z + k, NZ)
        return remote(
            cz_s.at[:, pl.ds(pl.multiple_of(peer * part, part), part)], cz_r.at[k - 1],
            cz_send.at[k - 1], cz_recv.at[k - 1], z_peer(k),
        )

    for k in range(1, NZ):
        cz_copy(k).start()

    owner_part(NBLK - 1)
    for j in range(2, NBLK - 1):
        back_product(j, back(j))

    for k in range(1, NZ):
        cz_copy(k).wait()
    own = cz_s[:, pl.ds(pl.multiple_of(z * part, part), part)] + cz_r[0] + cz_r[1] + cz_r[2]
    own = jnp.concatenate([own, jnp.zeros((128 - 40, part), F32)], axis=0)
    cp_s[...] = jnp.transpose(own).reshape(NP, 8, 128)

    def cp_copy(k):
        return remote(cp_s.at[lax.rem(me + k, NP)], cp_r.at[k - 1], cp_send, cp_recv, p_peer(k))

    def send_cp(k, carry):
        cp_copy(k).start()
        return carry

    weights = back(NBLK - 1)

    def q_copy(k):
        return remote(q_acc, q_r.at[k - 1], q_send.at[k - 1], q_recv.at[k - 1], z_peer(k))

    for k in range(1, NZ):
        q_copy(k).start()
    back_product(NBLK - 1, weights)
    g_s[...] = (g_acc[...] * (1.0 / VARIANTS)).astype(BF16)

    def g_copy(k):
        peer = lax.rem(z + k, NZ)
        return remote(
            g_s.at[:, pl.ds(pl.multiple_of(peer * QUARTER, QUARTER), QUARTER)], g_r.at[k - 1],
            g_send.at[k - 1], g_recv.at[k - 1], z_peer(k),
        )

    for k in range(1, NZ):
        g_copy(k).start()
    lax.fori_loop(1, NP, send_cp, 0)

    for k in range(1, NZ):
        q_copy(k).wait()
    q = q_acc[...]
    square = (q[0:1] + q_r[0, 0:1] + q_r[1, 0:1] + q_r[2, 0:1])[:, :RHS]
    res_norm = q[2:3, :RHS] * (1.0 / (2 * NBLK))
    dir_norm = q[3:4, :RHS] * (1.0 / (2 * NBLK))
    curvature = noise[...] * dir_norm + square * (1.0 / VARIANTS)
    step_row = res_norm / (curvature + 1e-6)
    step_col = to_column(step_row)
    s_next = s + step_col * d
    sol_new[...] = s_next
    s_sum = jnp.sum(s_next, axis=1, keepdims=True)
    s_square = jnp.sum(s_next * s_next, axis=1, keepdims=True)
    own_g = g_acc[:, pl.ds(pl.multiple_of(z * QUARTER, QUARTER), QUARTER)] * (1.0 / VARIANTS)
    base = to_column(noise[...]) * d + own_g
    for k in range(1, NZ):
        g_copy(k).wait()
    applied = base + g_r[0].astype(F32) + g_r[1].astype(F32) + g_r[2].astype(F32)
    r_next = r - step_col * applied
    res_new[...] = r_next
    r_square = jnp.sum(r_next * r_next, axis=1, keepdims=True)
    d1_s[...] = spread_columns((r_square, s_sum, s_square))

    def d1_copy(k):
        return remote(d1_s, d1_r.at[k - 1], d1_send.at[k - 1], d1_recv.at[k - 1], d1_peer(k))

    for k in range(1, 8):
        d1_copy(k).start()
    pltpu.make_async_copy(cp_r, cp_r, cp_recv).wait()
    dose = cp_s[me] + jnp.sum(cp_r[...], axis=0)
    for k in range(1, 8):
        d1_copy(k).wait()
    d2_s[...] = d1_s[...] + jnp.sum(d1_r[...], axis=0)

    def d2_copy(k):
        return remote(
            d2_s, d2_r.at[k - 1], d2_send, d2_recv, {"var": z, "samp": lax.rem(me + 2 * k, NP)}
        )

    def send_d2(k, carry):
        d2_copy(k).start()
        return carry

    lax.fori_loop(1, NP // 2, send_d2, 0)
    dose_freq = (dose[:, 32:33] * (1.0 / 100.0) + 1.0) / (2.0 * SAMPLES + 2.0)
    dose_spread = jnp.sqrt(2.0 * dose_freq * (1.0 - dose_freq))
    cross_sum = dose[:, 0:RHS] + step_row * dose[:, RHS:2 * RHS]
    pltpu.make_async_copy(d2_r, d2_r, d2_recv).wait()
    sums = jnp.sum(d2_s[...] + jnp.sum(d2_r[...], axis=0), axis=0, keepdims=True)
    beta = to_column(sums[:, 0:RHS] / (res_norm + 1e-6))
    dir_new[...] = r_next + beta * d
    scale = math.sqrt(SAMPLES) * jnp.sqrt(sums[:, 2 * RHS:3 * RHS] * (1.0 / SAMPLES) + 1e-6)
    scores[...] = (cross_sum * (1.0 / 100.0) - 2.0 * dose_freq * sums[:, RHS:2 * RHS]) / (dose_spread * scale)

    pltpu.make_async_copy(d2_r, d2_r, d2_send).wait()
    pltpu.make_async_copy(cp_r, cp_r, cp_send).wait()

    def sent(j, carry):
        for group in range(2):
            @pl.when(me != owner_of(j, group))
            def _():
                rs_copy(j, group).wait_send()

            @pl.when(me == owner_of(j, group))
            def _():
                view = rs_r.at[:, pl.ds(0, 16), :]
                pltpu.make_async_copy(view, view, ag_send).wait()

        return carry

    lax.fori_loop(0, NBLK, sent, 0)


def body(genotypes, called, dosage, sample_order, noise_ratio, solution, residual, direction):
    vmem = pl.BlockSpec(memory_space=pltpu.VMEM)
    hbm = pl.BlockSpec(memory_space=pl.ANY)
    dma = pltpu.SemaphoreType.DMA
    small = jax.ShapeDtypeStruct((RHS, QUARTER), F32)
    outs = pl.pallas_call(
        kernel,
        out_shape=(small, small, small, jax.ShapeDtypeStruct((8, RHS), F32)),
        in_specs=[hbm] * 3 + [vmem] * 5,
        out_specs=(vmem,) * 4,
        scratch_shapes=[
            pltpu.VMEM((NBLK, BLK, WIDE), jnp.int32),
            pltpu.VMEM((NBLK, BLK, WIDE), jnp.int32),
            pltpu.VMEM((QUARTER, IMPUTED), jnp.int32),
            pltpu.VMEM((NBLK, 2 * BLK, WIDE), BF16),
            pltpu.VMEM((2 * RHS, WIDE), BF16),
            pltpu.VMEM((QUARTER, IMPUTED), BF16),
            pltpu.VMEM((QUARTER, QUARTER), BF16),
            pltpu.VMEM((8, 128), F32),
            pltpu.VMEM((NZ - 1, 8, 128), F32),
            pltpu.VMEM((NBLK, 2, 24, 128), F32),
            pltpu.VMEM((NP - 1, 24, 128), F32),
            pltpu.VMEM((8, 128), F32),
            pltpu.VMEM((NBLK, 2, 32, 128), BF16),
            pltpu.VMEM((RHS, WIDE), F32),
            pltpu.VMEM((RHS, WIDE), BF16),
            pltpu.VMEM((NZ - 1, RHS, QUARTER), BF16),
            pltpu.VMEM((8, 128), F32),
            pltpu.VMEM((NZ - 1, 8, 128), F32),
            pltpu.VMEM((40, IMPUTED), F32),
            pltpu.VMEM((NZ - 1, 40, IMPUTED // NZ), F32),
            pltpu.VMEM((NP, 8, 128), F32),
            pltpu.VMEM((NP - 1, 8, 128), F32),
            pltpu.VMEM((8, 128), F32),
            pltpu.VMEM((7, 8, 128), F32),
            pltpu.VMEM((8, 128), F32),
            pltpu.VMEM((NP // 2 - 1, 8, 128), F32),
            dma((2, NBLK + 1)),
            dma((3,)), dma((3,)),
            dma((3,)), dma((3,)),
            dma((NBLK, 2)), dma,
            dma, dma((NBLK, 2)),
            dma((3,)), dma((3,)),
            dma((3,)), dma((3,)),
            dma((3,)), dma((3,)),
            dma, dma,
            dma((7,)), dma((7,)),
            dma, dma,
        ],
        compiler_params=pltpu.CompilerParams(
            collective_id=0, has_side_effects=True, vmem_limit_bytes=56 * 1024 * 1024
        ),
        cost_estimate=pl.CostEstimate(flops=400_000_000, bytes_accessed=22_000_000, transcendentals=0),
        name="cg_step",
    )(
        genotypes, called, dosage, sample_order, noise_ratio.reshape(1, RHS),
        solution.T, residual.T, direction.T,
    )
    sol_new, res_new, dir_new, scores = outs
    return (sol_new.T, res_new.T, dir_new.T, scores)


def solution(mesh):
    rows = P(("samp", "var"), None)
    return jax.shard_map(
        body,
        mesh=mesh,
        in_specs=(P("var", "samp"), P("var", "samp"), rows, rows, P(), rows, rows, rows),
        out_specs=(rows, rows, rows, P(("var", "samp"), None)),
        check_vma=False,
    )
```

```python
import math

import jax
import jax.numpy as jnp
from jax import lax
from jax.experimental import pallas as pl
from jax.experimental.pallas import tpu as pltpu
from jax.sharding import PartitionSpec as P

VARIANTS = 3072
SAMPLES = 98304
IMPUTED = 1024
RHS = 16
NZ = 4
NP = 32
QUARTER = 768
WIDE = QUARTER * NZ
LOCAL = VARIANTS // NZ
BLK = 128
NBLK = LOCAL // BLK
WINDOW = 3
EARLY = 3
F32 = jnp.float32
BF16 = jnp.bfloat16
MESH = pl.DeviceIdType.MESH


def owner_of(block, group):
    far = block + 10 - 4 * lax.rem(block // 2, 2)
    return 2 * (block + group * (far - block)) + group


def rows_iota(shape):
    return lax.broadcasted_iota(jnp.int32, shape, 0)


def lanes_iota(shape):
    return lax.broadcasted_iota(jnp.int32, shape, 1)


def to_column(row):
    eye = rows_iota((RHS, RHS)) == lanes_iota((RHS, RHS))
    return jnp.sum(jnp.where(eye, jnp.broadcast_to(row, (RHS, RHS)), 0.0), axis=1, keepdims=True)


def spread_columns(columns):
    rows, lanes = rows_iota((RHS, 128)), lanes_iota((RHS, 128))
    total = jnp.zeros((RHS, 128), F32)
    for k, column in enumerate(columns):
        total = jnp.where(lanes == rows + RHS * k, column, total)
    return total[:8] + total[8:]


def kernel(
    gen, cal, dos, order_in, noise_in, sol_in, res_in, dir_in,
    sol_new, res_new, dir_new, scores,
    order, noise, sol, res, dirn, gv, cv, dv, xb, dx, db, hot, stat_s, stat_r, rs_s, rs_r, ag_r, sq_r, g_acc, g_s, g_r,
    q_acc, q_r, cz_s, cz_r, cp_s, cp_r, d1_s, d1_r, d2_s, d2_r,
    in_sem, load_sem, a_send, a_recv, st_send, st_recv, rs_send, rs_recv, ag_send, ag_recv,
    sq_send, sq_recv,
    g_send, g_recv, q_send, q_recv, cz_send, cz_recv, cp_send, cp_recv, d1_send, d1_recv, d2_send, d2_recv,
):
    z = lax.axis_index("var")
    me = lax.axis_index("samp")

    def z_peer(k):
        return {"var": lax.rem(z + k, NZ), "samp": me}

    def p_peer(k):
        return {"var": z, "samp": lax.rem(me + k, NP)}

    def each_block(first, last, work):
        lax.fori_loop(first, last, lambda j, carry: (work(j), carry)[1], 0)

    def each_plane_peer(send):
        for first in (16, 8, 24, 0):
            lax.fori_loop(max(first, 1), first + 8, lambda k, carry: (send(k), carry)[1], 0)

    def remote(src, dst, send, recv, device):
        return pltpu.make_async_remote_copy(
            src_ref=src, dst_ref=dst, send_sem=send, recv_sem=recv, device_id=device, device_id_type=MESH
        )

    def load(j, which):
        source, target = ((gen, gv), (cal, cv))[which]
        return pltpu.make_async_copy(
            source.at[pl.ds(pl.multiple_of(j * BLK, BLK), BLK), :], target.at[j], load_sem.at[which, j]
        )

    load_dos = pltpu.make_async_copy(dos, dv, load_sem.at[0, NBLK])

    smalls = [
        pltpu.make_async_copy(source, target, in_sem.at[i])
        for i, (source, target) in enumerate(
            ((dir_in, dirn), (res_in, res), (sol_in, sol), (noise_in, noise), (order_in, order))
        )
    ]
    for copy in smalls:
        copy.start()
    for j in range(WINDOW):
        load(j, 0).start()
        load(j, 1).start()

    barrier = pltpu.get_barrier_semaphore()

    def greet(device):
        pl.semaphore_signal(barrier, inc=1, device_id=device, device_id_type=MESH)

    for k in range(1, NZ):
        greet(z_peer(k))
    each_plane_peer(lambda k: greet(p_peer(k)))
    for copy in smalls:
        copy.wait()

    d = dirn[...]
    r = res[...]
    d_b = d.astype(BF16)
    dx[:RHS, pl.ds(pl.multiple_of(z * QUARTER, QUARTER), QUARTER)] = d_b
    dx[RHS:, :] = jnp.ones((RHS, WIDE), BF16)
    r_col = jnp.sum(r * r, axis=1, keepdims=True)
    d_col = jnp.sum(d * d, axis=1, keepdims=True)
    row8, lane8 = rows_iota((8, 128)), lanes_iota((8, 128))
    pair = jnp.sum(spread_columns((jnp.zeros_like(r_col), r_col, d_col)), axis=0, keepdims=True)
    stat_s[...] = jnp.where(row8 == 2, pair, 0.0)
    g_acc[...] = jnp.zeros((RHS, WIDE), F32)

    pl.semaphore_wait(barrier, NP - 1 + NZ - 1)

    def direction_copy(k):
        mine = dx.at[pl.ds(0, RHS), pl.ds(pl.multiple_of(z * QUARTER, QUARTER), QUARTER)]
        return remote(mine, mine, a_send.at[k - 1], a_recv.at[k - 1], z_peer(k))

    def stat_copy(k):
        return remote(stat_s, stat_r.at[k - 1], st_send.at[k - 1], st_recv.at[k - 1], z_peer(k))

    for k in range(1, NZ):
        direction_copy(k).start()
        stat_copy(k).start()
    def rs_copy(j, group):
        owner = owner_of(j, group)
        slot = lax.rem(me - owner + NP - 1 + NP, NP)
        return remote(
            rs_s.at[j, group], rs_r.at[slot], rs_send.at[j, group], rs_recv, {"var": z, "samp": owner}
        )

    def convert_block(j):
        load(j, 0).wait()
        load(j, 1).wait()

        @pl.when(j + WINDOW < NBLK)
        def _():
            load(j + WINDOW, 0).start()
            load(j + WINDOW, 1).start()

        @pl.when(j + WINDOW == NBLK)
        def _():
            load_dos.start()

        def convert(i, carry):
            first = pl.multiple_of(i * 16, 16)
            called = cv[j, pl.ds(first, 16), :].astype(F32).astype(BF16)
            codes = gv[j, pl.ds(first, 16), :].astype(F32).astype(BF16)
            xb[j, pl.ds(first, 16), :] = codes * called
            xb[j, pl.ds(pl.multiple_of(first + BLK, 16), 16), :] = called
            return carry

        lax.fori_loop(0, BLK // 16, convert, 0)

    def project_block(j, stats):
        proj = lax.dot_general(dx[...], xb[j], (((1,), (1,)), ((), ())), preferred_element_type=F32)
        counts = jnp.where(row8 == 0, proj[16:24, :BLK], jnp.where(row8 == 1, proj[16:24, BLK:], stats))
        for group in range(2):
            rs_s[j, group, 0:8, :] = proj[8 * group:8 * group + 8, :BLK]
            rs_s[j, group, 8:16, :] = proj[8 * group:8 * group + 8, BLK:]
            rs_s[j, group, 16:24, :] = counts

            @pl.when(me != owner_of(j, group))
            def _():
                rs_copy(j, group).start()

    def ag_copy(j, group, k):
        return remote(ag_r.at[j, group], ag_r.at[j, group], ag_send, ag_recv.at[j, group], p_peer(k))

    def sq_copy(j, group, k):
        return remote(sq_r.at[j, group], sq_r.at[j, group], sq_send, sq_recv.at[j, group], p_peer(k))

    def owner_part(j):
        first, second = owner_of(j, 0), owner_of(j, 1)

        @pl.when((me == first) | (me == second))
        def _():
            group = (me == second).astype(jnp.int32)
            pltpu.make_async_copy(rs_r, rs_r, rs_recv).wait()
            total = rs_s[j, group] + jnp.sum(rs_r[...], axis=0)
            raw, called = total[0:8], total[8:16]
            frequency = (total[16:17] + 1.0) / (2.0 * total[17:18] + 2.0)
            spread = jnp.sqrt(2.0 * frequency * (1.0 - frequency))
            loading = (raw - 2.0 * frequency * called) / spread
            scaled_a = loading / spread
            scaled_b = 2.0 * frequency * loading / spread
            ag_r[j, group] = jnp.concatenate([scaled_a, -scaled_b], axis=0).astype(BF16)
            each_plane_peer(lambda k: ag_copy(j, group, k).start())
            square = jnp.sum(loading * loading, axis=1, keepdims=True)
            square = jnp.sum(jnp.where(lane8 == row8 + 8 * group, square, 0.0), axis=0, keepdims=True)
            sq_r[j, group] = square + jnp.where(lane8[:1] >= RHS, total[18:19], 0.0)
            each_plane_peer(lambda k: sq_copy(j, group, k).start())

    def back(j):
        halves = []
        for group in range(2):
            @pl.when(me != owner_of(j, group))
            def _():
                ag_copy(j, group, 1).wait_recv()

            halves.append(ag_r[j, group].astype(F32))
        left = jnp.concatenate([half[0:8] for half in halves], axis=0)
        right = jnp.concatenate([half[8:16] for half in halves], axis=0)
        weights = jnp.concatenate([left, right], axis=1).astype(BF16)
        return weights

    def back_product(j, weights):
        g_acc[...] += jnp.dot(weights, xb[j], preferred_element_type=F32)

    each_block(0, EARLY, convert_block)
    for k in range(1, NZ):
        stat_copy(k).wait()
    stats = stat_s[...] + stat_r[0] + stat_r[1] + stat_r[2]
    for k in range(1, NZ):
        direction_copy(k).wait()
    each_block(0, EARLY, lambda j: project_block(j, stats))

    def convert_and_project(j):
        convert_block(j)
        project_block(j, stats)

    each_block(EARLY, NBLK, convert_and_project)
    each_block(0, NBLK - 2, owner_part)

    load_dos.wait()

    def one_hot(i, carry):
        first = pl.multiple_of(i * 16, 16)
        hot[pl.ds(first, 16), :] = jnp.where(rows_iota((16, QUARTER)) + first == order[...], 1.0, 0.0).astype(BF16)
        return carry

    lax.fori_loop(0, QUARTER // 16, one_hot, 0)

    def convert_dose(i, carry):
        first = pl.multiple_of(i * 16, 16)
        db[pl.ds(first, 16), :] = dv[pl.ds(first, 16), :].astype(F32).astype(BF16)
        return carry

    lax.fori_loop(0, QUARTER // 16, convert_dose, 0)
    s = sol[...]
    s_high = s.astype(BF16)
    s_low = (s - s_high.astype(F32)).astype(BF16)
    d_low = (d - d_b.astype(F32)).astype(BF16)
    parts = jnp.concatenate([s_high, s_low, d_b, d_low], axis=0)
    picked = jnp.dot(parts, hot[...], preferred_element_type=F32).astype(BF16)
    picked = jnp.concatenate([picked, jnp.ones((RHS, QUARTER), BF16)], axis=0)
    cross = jnp.dot(picked, db[...], preferred_element_type=F32)
    cz_s[0:16, :] = cross[0:16] + cross[16:32]
    cz_s[16:32, :] = cross[32:48] + cross[48:64]
    cz_s[32:40, :] = cross[64:72]
    part = IMPUTED // NZ

    def cz_copy(k):
        peer = lax.rem(z + k, NZ)
        return remote(
            cz_s.at[:, pl.ds(pl.multiple_of(peer * part, part), part)], cz_r.at[k - 1],
            cz_send.at[k - 1], cz_recv.at[k - 1], z_peer(k),
        )

    for k in range(1, NZ):
        cz_copy(k).start()

    each_block(NBLK - 2, NBLK, owner_part)
    each_block(0, NBLK - 1, lambda j: back_product(j, back(j)))

    for k in range(1, NZ):
        cz_copy(k).wait()
    own = cz_s[:, pl.ds(pl.multiple_of(z * part, part), part)] + cz_r[0] + cz_r[1] + cz_r[2]
    own = jnp.concatenate([own, jnp.zeros((128 - 40, part), F32)], axis=0)
    cp_s[...] = jnp.transpose(own).reshape(NP, 8, 128)

    def cp_copy(k):
        return remote(cp_s.at[lax.rem(me + k, NP)], cp_r.at[k - 1], cp_send, cp_recv, p_peer(k))

    each_plane_peer(lambda k: cp_copy(k).start())
    weights = back(NBLK - 1)

    for j in range(NBLK):
        for group in range(2):
            @pl.when(me != owner_of(j, group))
            def _():
                sq_copy(j, group, 1).wait_recv()

    q_acc[...] = jnp.sum(sq_r[...], axis=(0, 1))

    def q_copy(k):
        return remote(q_acc, q_r.at[k - 1], q_send.at[k - 1], q_recv.at[k - 1], z_peer(k))

    for k in range(1, NZ):
        q_copy(k).start()
    back_product(NBLK - 1, weights)
    g_s[...] = (g_acc[...] * (1.0 / VARIANTS)).astype(BF16)

    def g_copy(k):
        peer = lax.rem(z + k, NZ)
        return remote(
            g_s.at[:, pl.ds(pl.multiple_of(peer * QUARTER, QUARTER), QUARTER)], g_r.at[k - 1],
            g_send.at[k - 1], g_recv.at[k - 1], z_peer(k),
        )

    for k in range(1, NZ):
        g_copy(k).start()

    for k in range(1, NZ):
        q_copy(k).wait()
    q = q_acc[...]
    square = (q + q_r[0] + q_r[1] + q_r[2])[:, :RHS]
    res_norm = q[:, RHS:2 * RHS] * (1.0 / (2 * NBLK))
    dir_norm = q[:, 2 * RHS:3 * RHS] * (1.0 / (2 * NBLK))
    curvature = noise[...] * dir_norm + square * (1.0 / VARIANTS)
    step_row = res_norm / (curvature + 1e-6)
    step_col = to_column(step_row)
    s_next = s + step_col * d
    sol_new[...] = s_next
    s_sum = jnp.sum(s_next, axis=1, keepdims=True)
    s_square = jnp.sum(s_next * s_next, axis=1, keepdims=True)
    own_g = g_acc[:, pl.ds(pl.multiple_of(z * QUARTER, QUARTER), QUARTER)] * (1.0 / VARIANTS)
    base = to_column(noise[...]) * d + own_g
    for k in range(1, NZ):
        g_copy(k).wait()
    applied = base + g_r[0].astype(F32) + g_r[1].astype(F32) + g_r[2].astype(F32)
    r_next = r - step_col * applied
    res_new[...] = r_next
    r_square = jnp.sum(r_next * r_next, axis=1, keepdims=True)
    d1_s[...] = spread_columns((r_square, s_sum, s_square))

    def d1_copy(k):
        return remote(d1_s, d1_r.at[k - 1], d1_send.at[k - 1], d1_recv.at[k - 1], z_peer(k))

    for k in range(1, NZ):
        d1_copy(k).start()
    pltpu.make_async_copy(cp_r, cp_r, cp_recv).wait()
    dose = cp_s[me] + jnp.sum(cp_r[...], axis=0)
    for k in range(1, NZ):
        d1_copy(k).wait()
    d2_s[...] = jnp.sum(d1_s[...] + jnp.sum(d1_r[...], axis=0), axis=0, keepdims=True)

    def d2_copy(k):
        return remote(d2_s, d2_r.at[k - 1], d2_send, d2_recv, p_peer(k))

    each_plane_peer(lambda k: d2_copy(k).start())
    dose_freq = (dose[:, 32:33] * (1.0 / 100.0) + 1.0) / (2.0 * SAMPLES + 2.0)
    dose_spread = jnp.sqrt(2.0 * dose_freq * (1.0 - dose_freq))
    cross_sum = dose[:, 0:RHS] + step_row * dose[:, RHS:2 * RHS]
    pltpu.make_async_copy(d2_r, d2_r, d2_recv).wait()
    sums = d2_s[...] + jnp.sum(d2_r[...], axis=0)
    beta = to_column(sums[:, 0:RHS] / (res_norm + 1e-6))
    dir_new[...] = r_next + beta * d
    scale = math.sqrt(SAMPLES) * jnp.sqrt(sums[:, 2 * RHS:3 * RHS] * (1.0 / SAMPLES) + 1e-6)
    scores[...] = (cross_sum * (1.0 / 100.0) - 2.0 * dose_freq * sums[:, RHS:2 * RHS]) / (dose_spread * scale)

    pltpu.make_async_copy(d2_r, d2_r, d2_send).wait()
    pltpu.make_async_copy(cp_r, cp_r, cp_send).wait()

    def sent(j, carry):
        for group in range(2):
            @pl.when(me != owner_of(j, group))
            def _():
                rs_copy(j, group).wait_send()

            @pl.when(me == owner_of(j, group))
            def _():
                view = rs_r.at[:, pl.ds(0, 8), :]
                pltpu.make_async_copy(view, view, ag_send).wait()
                pltpu.make_async_copy(d2_r, d2_r, sq_send).wait()

        return carry

    lax.fori_loop(0, NBLK, sent, 0)


def body(genotypes, called, dosage, sample_order, noise_ratio, solution, residual, direction):
    vmem = pl.BlockSpec(memory_space=pltpu.VMEM)
    hbm = pl.BlockSpec(memory_space=pltpu.HBM)
    dma = pltpu.SemaphoreType.DMA
    small = jax.ShapeDtypeStruct((RHS, QUARTER), F32)
    outs = pl.pallas_call(
        kernel,
        out_shape=(pltpu.VMEM((RHS, QUARTER), F32),) * 3 + (pltpu.VMEM((8, RHS), F32),),
        in_specs=[hbm] * 8,
        out_specs=(vmem,) * 4,
        scratch_shapes=[
            pltpu.VMEM((1, QUARTER), jnp.int32),
            pltpu.VMEM((1, RHS), F32),
            pltpu.VMEM((RHS, QUARTER), F32),
            pltpu.VMEM((RHS, QUARTER), F32),
            pltpu.VMEM((RHS, QUARTER), F32),
            pltpu.VMEM((NBLK, BLK, WIDE), jnp.int32),
            pltpu.VMEM((NBLK, BLK, WIDE), jnp.int32),
            pltpu.VMEM((QUARTER, IMPUTED), jnp.int32),
            pltpu.VMEM((NBLK, 2 * BLK, WIDE), BF16),
            pltpu.VMEM((2 * RHS, WIDE), BF16),
            pltpu.VMEM((QUARTER, IMPUTED), BF16),
            pltpu.VMEM((QUARTER, QUARTER), BF16),
            pltpu.VMEM((8, 128), F32),
            pltpu.VMEM((NZ - 1, 8, 128), F32),
            pltpu.VMEM((NBLK, 2, 24, 128), F32),
            pltpu.VMEM((NP - 1, 24, 128), F32),
            pltpu.VMEM((NBLK, 2, 16, 128), BF16),
            pltpu.VMEM((NBLK, 2, 1, 128), F32),
            pltpu.VMEM((RHS, WIDE), F32),
            pltpu.VMEM((RHS, WIDE), BF16),
            pltpu.VMEM((NZ - 1, RHS, QUARTER), BF16),
            pltpu.VMEM((1, 128), F32),
            pltpu.VMEM((NZ - 1, 1, 128), F32),
            pltpu.VMEM((40, IMPUTED), F32),
            pltpu.VMEM((NZ - 1, 40, IMPUTED // NZ), F32),
            pltpu.VMEM((NP, 8, 128), F32),
            pltpu.VMEM((NP - 1, 8, 128), F32),
            pltpu.VMEM((8, 128), F32),
            pltpu.VMEM((NZ - 1, 8, 128), F32),
            pltpu.VMEM((1, 128), F32),
            pltpu.VMEM((NP - 1, 1, 128), F32),
            dma((5,)),
            dma((2, NBLK + 1)),
            dma((3,)), dma((3,)),
            dma((3,)), dma((3,)),
            dma((NBLK, 2)), dma,
            dma, dma((NBLK, 2)),
            dma, dma((NBLK, 2)),
            dma((3,)), dma((3,)),
            dma((3,)), dma((3,)),
            dma((3,)), dma((3,)),
            dma, dma,
            dma((3,)), dma((3,)),
            dma, dma,
        ],
        compiler_params=pltpu.CompilerParams(
            collective_id=0, has_side_effects=True, vmem_limit_bytes=56 * 1024 * 1024
        ),
        cost_estimate=pl.CostEstimate(flops=400_000_000, bytes_accessed=22_000_000, transcendentals=0),
        name="cg_step",
    )(
        genotypes, called, dosage, sample_order, noise_ratio.reshape(1, RHS),
        solution.T, residual.T, direction.T,
    )
    sol_new, res_new, dir_new, scores = outs
    return (sol_new.T, res_new.T, dir_new.T, scores)


def solution(mesh):
    rows = P(("samp", "var"), None)
    return jax.shard_map(
        body,
        mesh=mesh,
        in_specs=(P("var", "samp"), P("var", "samp"), rows, rows, P(), rows, rows, rows),
        out_specs=(rows, rows, rows, P(("var", "samp"), None)),
        check_vma=False,
    )
```

```python
import math

import jax
import jax.numpy as jnp
from jax import lax
from jax.experimental import pallas as pl
from jax.experimental.pallas import tpu as pltpu
from jax.sharding import PartitionSpec as P

VARIANTS = 3072
SAMPLES = 98304
IMPUTED = 1024
RHS = 16
NZ = 4
NP = 32
QUARTER = 768
WIDE = QUARTER * NZ
LOCAL = VARIANTS // NZ
BLK = 128
NBLK = LOCAL // BLK
WINDOW = 3
F32 = jnp.float32
BF16 = jnp.bfloat16
MESH = pl.DeviceIdType.MESH


def owner_of(block, group):
    turn = block + 2
    first = lax.rem(turn, 4) + 4 * (1 - turn // 4)
    second = block + 7
    return 2 * (first + group * (second - first)) + group


def rows_iota(shape):
    return lax.broadcasted_iota(jnp.int32, shape, 0)


def lanes_iota(shape):
    return lax.broadcasted_iota(jnp.int32, shape, 1)


def to_column(row):
    eye = rows_iota((RHS, RHS)) == lanes_iota((RHS, RHS))
    return jnp.sum(jnp.where(eye, jnp.broadcast_to(row, (RHS, RHS)), 0.0), axis=1, keepdims=True)


def spread_columns(columns):
    rows, lanes = rows_iota((RHS, 128)), lanes_iota((RHS, 128))
    total = jnp.zeros((RHS, 128), F32)
    for k, column in enumerate(columns):
        total = jnp.where(lanes == rows + RHS * k, column, total)
    return total[:8] + total[8:]


def kernel(
    gen, cal, dos, order_in, noise_in, sol_in, res_in, dir_in,
    sol_new, res_new, dir_new, scores,
    order, noise, sol, res, dirn, gv, cv, dv, xb, dx, db, hot, stat_s, stat_r, rs_s, rs_r, ag_r, sq_r, g_acc, g_s, g_r,
    q_acc, q_r, cz_s, cz_r, cp_s, cp_r, d1_s, d1_r, d2_s, d2_r,
    in_sem, load_sem, a_send, a_recv, st_send, st_recv, rs_send, rs_recv, ag_send, ag_recv,
    sq_send, sq_recv,
    g_send, g_recv, q_send, q_recv, cz_send, cz_recv, cp_send, cp_recv, d1_send, d1_recv, d2_send, d2_recv,
):
    z = lax.axis_index("var")
    me = lax.axis_index("samp")

    def z_peer(k):
        return {"var": lax.rem(z + k, NZ), "samp": me}

    def p_peer(k):
        return {"var": z, "samp": lax.rem(me + k, NP)}

    def each_block(first, last, work):
        lax.fori_loop(first, last, lambda j, carry: (work(j), carry)[1], 0)

    def each_plane_peer(send):
        for first in (16, 8, 24, 0):
            lax.fori_loop(max(first, 1), first + 8, lambda k, carry: (send(k), carry)[1], 0)

    def remote(src, dst, send, recv, device):
        return pltpu.make_async_remote_copy(
            src_ref=src, dst_ref=dst, send_sem=send, recv_sem=recv, device_id=device, device_id_type=MESH
        )

    def load(j, which):
        source, target = ((gen, gv), (cal, cv))[which]
        return pltpu.make_async_copy(
            source.at[pl.ds(pl.multiple_of(j * BLK, BLK), BLK), :], target.at[j], load_sem.at[which, j]
        )

    load_dos = pltpu.make_async_copy(dos, dv, load_sem.at[0, NBLK])

    smalls = [
        pltpu.make_async_copy(source, target, in_sem.at[i])
        for i, (source, target) in enumerate(
            ((dir_in, dirn), (res_in, res), (sol_in, sol), (noise_in, noise), (order_in, order))
        )
    ]
    for copy in smalls:
        copy.start()
    for j in range(WINDOW):
        load(j, 0).start()
        load(j, 1).start()

    barrier = pltpu.get_barrier_semaphore()
    place = me // 8 + lax.rem(me // 2, 4) + 2 * z
    ahead = jnp.maximum(3 - place // 2, 0)
    early = jnp.maximum(6 - place // 3, 3)

    def greet(device):
        pl.semaphore_signal(barrier, inc=1, device_id=device, device_id_type=MESH)

    for k in range(1, NZ):
        greet(z_peer(k))
    each_plane_peer(lambda k: greet(p_peer(k)))
    for copy in smalls:
        copy.wait()

    d = dirn[...]
    r = res[...]
    d_b = d.astype(BF16)
    dx[:RHS, pl.ds(pl.multiple_of(z * QUARTER, QUARTER), QUARTER)] = d_b
    dx[RHS:, :] = jnp.ones((RHS, WIDE), BF16)
    r_col = jnp.sum(r * r, axis=1, keepdims=True)
    d_col = jnp.sum(d * d, axis=1, keepdims=True)
    row8, lane8 = rows_iota((8, 128)), lanes_iota((8, 128))
    pair = jnp.sum(spread_columns((jnp.zeros_like(r_col), r_col, d_col)), axis=0, keepdims=True)
    stat_s[...] = jnp.where(row8 == 2, pair, 0.0)
    g_acc[...] = jnp.zeros((RHS, WIDE), F32)

    def convert_block(j):
        load(j, 0).wait()
        load(j, 1).wait()

        @pl.when(j + WINDOW < NBLK)
        def _():
            load(j + WINDOW, 0).start()
            load(j + WINDOW, 1).start()

        @pl.when(j + WINDOW == NBLK)
        def _():
            load_dos.start()

        def convert(i, carry):
            first = pl.multiple_of(i * 16, 16)
            called = cv[j, pl.ds(first, 16), :].astype(F32).astype(BF16)
            codes = gv[j, pl.ds(first, 16), :].astype(F32).astype(BF16)
            xb[j, pl.ds(first, 16), :] = codes * called
            xb[j, pl.ds(pl.multiple_of(first + BLK, 16), 16), :] = called
            return carry

        lax.fori_loop(0, BLK // 16, convert, 0)

    each_block(0, ahead, convert_block)
    pl.semaphore_wait(barrier, NP - 1 + NZ - 1)

    def direction_copy(k):
        mine = dx.at[pl.ds(0, RHS), pl.ds(pl.multiple_of(z * QUARTER, QUARTER), QUARTER)]
        return remote(mine, mine, a_send.at[k - 1], a_recv.at[k - 1], z_peer(k))

    def stat_copy(k):
        return remote(stat_s, stat_r.at[k - 1], st_send.at[k - 1], st_recv.at[k - 1], z_peer(k))

    for k in range(1, NZ):
        direction_copy(k).start()
        stat_copy(k).start()
    def rs_copy(j, group):
        owner = owner_of(j, group)
        slot = lax.rem(me - owner + NP - 1 + NP, NP)
        return remote(
            rs_s.at[j, group], rs_r.at[slot], rs_send.at[j, group], rs_recv, {"var": z, "samp": owner}
        )

    def project_block(j, stats):
        proj = lax.dot_general(dx[...], xb[j], (((1,), (1,)), ((), ())), preferred_element_type=F32)
        counts = jnp.where(row8 == 0, proj[16:24, :BLK], jnp.where(row8 == 1, proj[16:24, BLK:], stats))
        for group in range(2):
            rs_s[j, group, 0:8, :] = proj[8 * group:8 * group + 8, :BLK]
            rs_s[j, group, 8:16, :] = proj[8 * group:8 * group + 8, BLK:]
            rs_s[j, group, 16:24, :] = counts

            @pl.when(me != owner_of(j, group))
            def _():
                rs_copy(j, group).start()

    def ag_copy(j, group, k):
        return remote(ag_r.at[j, group], ag_r.at[j, group], ag_send, ag_recv.at[j, group], p_peer(k))

    def sq_copy(j, group, k):
        return remote(sq_r.at[j, group], sq_r.at[j, group], sq_send, sq_recv.at[j, group], p_peer(k))

    def owner_part(j):
        first, second = owner_of(j, 0), owner_of(j, 1)

        @pl.when((me == first) | (me == second))
        def _():
            group = (me == second).astype(jnp.int32)
            pltpu.make_async_copy(rs_r, rs_r, rs_recv).wait()
            total = rs_s[j, group] + jnp.sum(rs_r[...], axis=0)
            raw, called = total[0:8], total[8:16]
            frequency = (total[16:17] + 1.0) / (2.0 * total[17:18] + 2.0)
            spread = jnp.sqrt(2.0 * frequency * (1.0 - frequency))
            loading = (raw - 2.0 * frequency * called) / spread
            scaled_a = loading / spread
            scaled_b = 2.0 * frequency * loading / spread
            ag_r[j, group] = jnp.concatenate([scaled_a, -scaled_b], axis=0).astype(BF16)
            each_plane_peer(lambda k: ag_copy(j, group, k).start())
            square = jnp.sum(loading * loading, axis=1, keepdims=True)
            square = jnp.sum(jnp.where(lane8 == row8 + 8 * group, square, 0.0), axis=0, keepdims=True)
            sq_r[j, group] = square + jnp.where(lane8[:1] >= RHS, total[18:19], 0.0)
            each_plane_peer(lambda k: sq_copy(j, group, k).start())

    def back(j):
        halves = []
        for group in range(2):
            @pl.when(me != owner_of(j, group))
            def _():
                ag_copy(j, group, 1).wait_recv()

            halves.append(ag_r[j, group].astype(F32))
        left = jnp.concatenate([half[0:8] for half in halves], axis=0)
        right = jnp.concatenate([half[8:16] for half in halves], axis=0)
        weights = jnp.concatenate([left, right], axis=1).astype(BF16)
        return weights

    def back_product(j, weights):
        g_acc[...] += jnp.dot(weights, xb[j], preferred_element_type=F32)

    each_block(ahead, early, convert_block)
    for k in range(1, NZ):
        stat_copy(k).wait()
    stats = stat_s[...] + stat_r[0] + stat_r[1] + stat_r[2]
    for k in range(1, NZ):
        direction_copy(k).wait()
    each_block(0, early, lambda j: project_block(j, stats))

    def convert_and_project(j):
        convert_block(j)
        project_block(j, stats)

    each_block(early, NBLK, convert_and_project)
    each_block(0, NBLK, owner_part)

    load_dos.wait()

    def one_hot(i, carry):
        first = pl.multiple_of(i * 16, 16)
        hot[pl.ds(first, 16), :] = jnp.where(rows_iota((16, QUARTER)) + first == order[...], 1.0, 0.0).astype(BF16)
        return carry

    lax.fori_loop(0, QUARTER // 16, one_hot, 0)

    def convert_dose(i, carry):
        first = pl.multiple_of(i * 16, 16)
        db[pl.ds(first, 16), :] = dv[pl.ds(first, 16), :].astype(F32).astype(BF16)
        return carry

    lax.fori_loop(0, QUARTER // 16, convert_dose, 0)
    s = sol[...]
    s_high = s.astype(BF16)
    s_low = (s - s_high.astype(F32)).astype(BF16)
    d_low = (d - d_b.astype(F32)).astype(BF16)
    parts = jnp.concatenate([s_high, s_low, d_b, d_low], axis=0)
    picked = jnp.dot(parts, hot[...], preferred_element_type=F32).astype(BF16)
    picked = jnp.concatenate([picked, jnp.ones((RHS, QUARTER), BF16)], axis=0)
    cross = jnp.dot(picked, db[...], preferred_element_type=F32)
    cz_s[0:16, :] = cross[0:16] + cross[16:32]
    cz_s[16:32, :] = cross[32:48] + cross[48:64]
    cz_s[32:40, :] = cross[64:72]
    part = IMPUTED // NZ

    def cz_copy(k):
        peer = lax.rem(z + k, NZ)
        return remote(
            cz_s.at[:, pl.ds(pl.multiple_of(peer * part, part), part)], cz_r.at[k - 1],
            cz_send.at[k - 1], cz_recv.at[k - 1], z_peer(k),
        )

    for k in range(1, NZ):
        cz_copy(k).start()

    each_block(0, NBLK - 1, lambda j: back_product(j, back(j)))

    weights = back(NBLK - 1)

    for j in range(NBLK):
        for group in range(2):
            @pl.when(me != owner_of(j, group))
            def _():
                sq_copy(j, group, 1).wait_recv()

    q_acc[...] = jnp.sum(sq_r[...], axis=(0, 1))

    def q_copy(k):
        return remote(q_acc, q_r.at[k - 1], q_send.at[k - 1], q_recv.at[k - 1], z_peer(k))

    for k in range(1, NZ):
        q_copy(k).start()
    def g_copy(k):
        peer = lax.rem(z + k, NZ)
        return remote(
            g_s.at[:, pl.ds(pl.multiple_of(peer * QUARTER, QUARTER), QUARTER)], g_r.at[k - 1],
            g_send.at[k - 1], g_recv.at[k - 1], z_peer(k),
        )

    for k in (2, 1, 3, 0):
        span = pl.ds(pl.multiple_of(lax.rem(z + k, NZ) * QUARTER, QUARTER), QUARTER)
        g_part = (
            g_acc[:, span] + jnp.dot(weights, xb[NBLK - 1, :, span], preferred_element_type=F32)
        ) * (1.0 / VARIANTS)
        if k:
            g_s[:, span] = g_part.astype(BF16)
            g_copy(k).start()
        else:
            own_g = g_part

    for k in range(1, NZ):
        cz_copy(k).wait()
    own = cz_s[:, pl.ds(pl.multiple_of(z * part, part), part)] + cz_r[0] + cz_r[1] + cz_r[2]
    own = jnp.concatenate([own, jnp.zeros((128 - 40, part), F32)], axis=0)
    cp_s[...] = jnp.transpose(own).reshape(NP, 8, 128)

    def cp_copy(k):
        return remote(cp_s.at[lax.rem(me + k, NP)], cp_r.at[k - 1], cp_send, cp_recv, p_peer(k))

    each_plane_peer(lambda k: cp_copy(k).start())

    for k in range(1, NZ):
        q_copy(k).wait()
    q = q_acc[...]
    square = (q + q_r[0] + q_r[1] + q_r[2])[:, :RHS]
    res_norm = q[:, RHS:2 * RHS] * (1.0 / (2 * NBLK))
    dir_norm = q[:, 2 * RHS:3 * RHS] * (1.0 / (2 * NBLK))
    curvature = noise[...] * dir_norm + square * (1.0 / VARIANTS)
    step_row = res_norm / (curvature + 1e-6)
    step_col = to_column(step_row)
    s_next = s + step_col * d
    sol_new[...] = s_next
    s_sum = jnp.sum(s_next, axis=1, keepdims=True)
    s_square = jnp.sum(s_next * s_next, axis=1, keepdims=True)
    base = to_column(noise[...]) * d + own_g
    for k in range(1, NZ):
        g_copy(k).wait()
    applied = base + g_r[0].astype(F32) + g_r[1].astype(F32) + g_r[2].astype(F32)
    r_next = r - step_col * applied
    res_new[...] = r_next
    r_square = jnp.sum(r_next * r_next, axis=1, keepdims=True)
    d1_s[...] = spread_columns((r_square, s_sum, s_square))

    def d1_copy(k):
        return remote(d1_s, d1_r.at[k - 1], d1_send.at[k - 1], d1_recv.at[k - 1], z_peer(k))

    for k in range(1, NZ):
        d1_copy(k).start()
    pltpu.make_async_copy(cp_r, cp_r, cp_recv).wait()
    dose = cp_s[me] + jnp.sum(cp_r[...], axis=0)
    for k in range(1, NZ):
        d1_copy(k).wait()
    d2_s[...] = jnp.sum(d1_s[...] + jnp.sum(d1_r[...], axis=0), axis=0, keepdims=True)

    def d2_copy(k):
        return remote(d2_s, d2_r.at[k - 1], d2_send, d2_recv, p_peer(k))

    each_plane_peer(lambda k: d2_copy(k).start())
    dose_freq = (dose[:, 32:33] * (1.0 / 100.0) + 1.0) / (2.0 * SAMPLES + 2.0)
    dose_spread = jnp.sqrt(2.0 * dose_freq * (1.0 - dose_freq))
    cross_sum = dose[:, 0:RHS] + step_row * dose[:, RHS:2 * RHS]
    pltpu.make_async_copy(cp_r, cp_r, cp_send).wait()

    def sent(j, carry):
        for group in range(2):
            @pl.when(me != owner_of(j, group))
            def _():
                rs_copy(j, group).wait_send()

            @pl.when(me == owner_of(j, group))
            def _():
                view = rs_r.at[:, pl.ds(0, 8), :]
                pltpu.make_async_copy(view, view, ag_send).wait()
                pltpu.make_async_copy(d2_r, d2_r, sq_send).wait()

        return carry

    lax.fori_loop(0, NBLK, sent, 0)

    pltpu.make_async_copy(d2_r, d2_r, d2_recv).wait()
    sums = d2_s[...] + jnp.sum(d2_r[...], axis=0)
    beta = to_column(sums[:, 0:RHS] / (res_norm + 1e-6))
    dir_new[...] = r_next + beta * d
    scale = math.sqrt(SAMPLES) * jnp.sqrt(sums[:, 2 * RHS:3 * RHS] * (1.0 / SAMPLES) + 1e-6)
    scores[...] = (cross_sum * (1.0 / 100.0) - 2.0 * dose_freq * sums[:, RHS:2 * RHS]) / (dose_spread * scale)

    pltpu.make_async_copy(d2_r, d2_r, d2_send).wait()


def store_kernel(*refs):
    held, results, sem = refs[:4], refs[4:8], refs[8]
    copies = [pltpu.make_async_copy(held[i], results[i], sem.at[i]) for i in range(4)]
    for copy in copies:
        copy.start()
    for copy in copies:
        copy.wait()


def body(genotypes, called, dosage, sample_order, noise_ratio, solution, residual, direction):
    vmem = pl.BlockSpec(memory_space=pltpu.VMEM)
    hbm = pl.BlockSpec(memory_space=pltpu.HBM)
    dma = pltpu.SemaphoreType.DMA
    small = jax.ShapeDtypeStruct((RHS, QUARTER), F32)
    outs = pl.pallas_call(
        kernel,
        out_shape=(pltpu.VMEM((RHS, QUARTER), F32),) * 3 + (pltpu.VMEM((8, RHS), F32),),
        in_specs=[hbm] * 8,
        out_specs=(vmem,) * 4,
        scratch_shapes=[
            pltpu.VMEM((1, QUARTER), jnp.int32),
            pltpu.VMEM((1, RHS), F32),
            pltpu.VMEM((RHS, QUARTER), F32),
            pltpu.VMEM((RHS, QUARTER), F32),
            pltpu.VMEM((RHS, QUARTER), F32),
            pltpu.VMEM((NBLK, BLK, WIDE), jnp.int32),
            pltpu.VMEM((NBLK, BLK, WIDE), jnp.int32),
            pltpu.VMEM((QUARTER, IMPUTED), jnp.int32),
            pltpu.VMEM((NBLK, 2 * BLK, WIDE), BF16),
            pltpu.VMEM((2 * RHS, WIDE), BF16),
            pltpu.VMEM((QUARTER, IMPUTED), BF16),
            pltpu.VMEM((QUARTER, QUARTER), BF16),
            pltpu.VMEM((8, 128), F32),
            pltpu.VMEM((NZ - 1, 8, 128), F32),
            pltpu.VMEM((NBLK, 2, 24, 128), F32),
            pltpu.VMEM((NP - 1, 24, 128), F32),
            pltpu.VMEM((NBLK, 2, 16, 128), BF16),
            pltpu.VMEM((NBLK, 2, 1, 128), F32),
            pltpu.VMEM((RHS, WIDE), F32),
            pltpu.VMEM((RHS, WIDE), BF16),
            pltpu.VMEM((NZ - 1, RHS, QUARTER), BF16),
            pltpu.VMEM((1, 128), F32),
            pltpu.VMEM((NZ - 1, 1, 128), F32),
            pltpu.VMEM((40, IMPUTED), F32),
            pltpu.VMEM((NZ - 1, 40, IMPUTED // NZ), F32),
            pltpu.VMEM((NP, 8, 128), F32),
            pltpu.VMEM((NP - 1, 8, 128), F32),
            pltpu.VMEM((8, 128), F32),
            pltpu.VMEM((NZ - 1, 8, 128), F32),
            pltpu.VMEM((1, 128), F32),
            pltpu.VMEM((NP - 1, 1, 128), F32),
            dma((5,)),
            dma((2, NBLK + 1)),
            dma((3,)), dma((3,)),
            dma((3,)), dma((3,)),
            dma((NBLK, 2)), dma,
            dma, dma((NBLK, 2)),
            dma, dma((NBLK, 2)),
            dma((3,)), dma((3,)),
            dma((3,)), dma((3,)),
            dma((3,)), dma((3,)),
            dma, dma,
            dma((3,)), dma((3,)),
            dma, dma,
        ],
        compiler_params=pltpu.CompilerParams(
            collective_id=0, has_side_effects=True, vmem_limit_bytes=56 * 1024 * 1024
        ),
        cost_estimate=pl.CostEstimate(flops=400_000_000, bytes_accessed=22_000_000, transcendentals=0),
        name="cg_step",
    )(
        genotypes, called, dosage, sample_order, noise_ratio.reshape(1, RHS),
        solution.T, residual.T, direction.T,
    )
    outs = [pltpu.with_memory_space_constraint(out, pltpu.VMEM) for out in outs]
    sol_new, res_new, dir_new, scores = pl.pallas_call(
        store_kernel,
        out_shape=(small, small, small, jax.ShapeDtypeStruct((8, RHS), F32)),
        in_specs=[vmem] * 4,
        out_specs=(hbm,) * 4,
        scratch_shapes=[dma((4,))],
        cost_estimate=pl.CostEstimate(flops=0, bytes_accessed=300_000, transcendentals=0),
        name="store",
    )(*outs)
    return (sol_new.T, res_new.T, dir_new.T, scores)


def solution(mesh):
    rows = P(("samp", "var"), None)
    return jax.shard_map(
        body,
        mesh=mesh,
        in_specs=(P("var", "samp"), P("var", "samp"), rows, rows, P(), rows, rows, rows),
        out_specs=(rows, rows, rows, P(("var", "samp"), None)),
        check_vma=False,
    )
```

```python
import math

import jax
import jax.numpy as jnp
from jax import lax
from jax.experimental import pallas as pl
from jax.experimental.pallas import tpu as pltpu
from jax.sharding import PartitionSpec as P

VARIANTS = 3072
SAMPLES = 98304
IMPUTED = 1024
RHS = 16
NZ = 4
NP = 32
QUARTER = 768
WIDE = QUARTER * NZ
LOCAL = VARIANTS // NZ
BLK = 128
NBLK = LOCAL // BLK
WINDOW = 3
F32 = jnp.float32
BF16 = jnp.bfloat16
MESH = pl.DeviceIdType.MESH


def owner_of(block, group):
    turn = block + 2
    first = lax.rem(turn, 4) + 4 * (1 - turn // 4)
    second = block + 7
    return 2 * (first + group * (second - first)) + group


def rows_iota(shape):
    return lax.broadcasted_iota(jnp.int32, shape, 0)


def lanes_iota(shape):
    return lax.broadcasted_iota(jnp.int32, shape, 1)


def to_column(row):
    eye = rows_iota((RHS, RHS)) == lanes_iota((RHS, RHS))
    return jnp.sum(jnp.where(eye, jnp.broadcast_to(row, (RHS, RHS)), 0.0), axis=1, keepdims=True)


def spread_columns(columns):
    rows, lanes = rows_iota((RHS, 128)), lanes_iota((RHS, 128))
    total = jnp.zeros((RHS, 128), F32)
    for k, column in enumerate(columns):
        total = jnp.where(lanes == rows + RHS * k, column, total)
    return total[:8] + total[8:]


def kernel(
    gen, cal, dos, order_in, noise_in, sol_in, res_in, dir_in,
    sol_new, res_new, dir_new, scores,
    order, noise, sol, res, dirn, gv, cv, dv, xb, dx, db, hot, stat_s, stat_r, rs_s, rs_r, ag_r, sq_r, g_acc, g_s, g_r,
    q_acc, q_r, cz_s, cz_r, cp_s, cp_r, d1_s, d1_r, d2_s, d2_r,
    in_sem, load_sem, a_send, a_recv, st_send, st_recv, rs_send, rs_recv, ag_send, ag_recv,
    sq_send, sq_recv,
    g_send, g_recv, q_send, q_recv, cz_send, cz_recv, cp_send, cp_recv, d1_send, d1_recv, d2_send, d2_recv,
):
    z = lax.axis_index("var")
    me = lax.axis_index("samp")

    def z_peer(k):
        return {"var": lax.rem(z + k, NZ), "samp": me}

    def beside(k):
        peer = me + k
        return jnp.where(peer >= NP, peer - NP, peer)

    def p_peer(k):
        return {"var": z, "samp": beside(k)}

    def each_block(first, last, work):
        lax.fori_loop(first, last, lambda j, carry: (work(j), carry)[1], 0)

    def each_plane_peer(send):
        for first in (16, 8, 24, 0):
            lax.fori_loop(max(first, 1), first + 8, lambda k, carry: (send(k), carry)[1], 0, unroll=True)

    def remote(src, dst, send, recv, device):
        return pltpu.make_async_remote_copy(
            src_ref=src, dst_ref=dst, send_sem=send, recv_sem=recv, device_id=device, device_id_type=MESH
        )

    def load(j, which):
        source, target = ((gen, gv), (cal, cv))[which]
        return pltpu.make_async_copy(
            source.at[pl.ds(pl.multiple_of(j * BLK, BLK), BLK), :], target.at[j], load_sem.at[which, j]
        )

    load_dos = pltpu.make_async_copy(dos, dv, load_sem.at[0, NBLK])

    smalls = [
        pltpu.make_async_copy(source, target, in_sem.at[i])
        for i, (source, target) in enumerate(
            ((dir_in, dirn), (res_in, res), (sol_in, sol), (noise_in, noise), (order_in, order))
        )
    ]
    for copy in smalls:
        copy.start()
    for j in range(WINDOW):
        load(j, 0).start()
        load(j, 1).start()

    barrier = pltpu.get_barrier_semaphore()
    place = me // 8 + lax.rem(me // 2, 4) + 2 * z
    ahead = jnp.maximum(3 - place // 2, 0)
    early = NBLK - z

    def greet(device):
        pl.semaphore_signal(barrier, inc=1, device_id=device, device_id_type=MESH)

    for k in range(1, NZ):
        greet(z_peer(k))
    each_plane_peer(lambda k: greet(p_peer(k)))
    for copy in smalls:
        copy.wait()

    d = dirn[...]
    r = res[...]
    d_b = d.astype(BF16)
    dx[:RHS, pl.ds(pl.multiple_of(z * QUARTER, QUARTER), QUARTER)] = d_b
    dx[RHS:, :] = jnp.ones((RHS, WIDE), BF16)
    r_col = jnp.sum(r * r, axis=1, keepdims=True)
    d_col = jnp.sum(d * d, axis=1, keepdims=True)
    row8, lane8 = rows_iota((8, 128)), lanes_iota((8, 128))
    pair = jnp.sum(spread_columns((jnp.zeros_like(r_col), r_col, d_col)), axis=0, keepdims=True)
    stat_s[...] = jnp.where(row8 == 2, pair, 0.0)
    g_acc[...] = jnp.zeros((RHS, WIDE), F32)

    def convert_block(j):
        load(j, 0).wait()
        load(j, 1).wait()

        @pl.when(j + WINDOW < NBLK)
        def _():
            load(j + WINDOW, 0).start()
            load(j + WINDOW, 1).start()

        @pl.when(j == NBLK - 1)
        def _():
            load_dos.start()

        def convert(i, carry):
            first = pl.multiple_of(i * 16, 16)
            called = cv[j, pl.ds(first, 16), :].astype(F32).astype(BF16)
            codes = gv[j, pl.ds(first, 16), :].astype(F32).astype(BF16)
            xb[j, pl.ds(first, 16), :] = codes * called
            xb[j, pl.ds(pl.multiple_of(first + BLK, 16), 16), :] = called
            return carry

        lax.fori_loop(0, BLK // 16, convert, 0)

    each_block(0, ahead, convert_block)
    pl.semaphore_wait(barrier, NP - 1 + NZ - 1)

    def direction_copy(k):
        mine = dx.at[pl.ds(0, RHS), pl.ds(pl.multiple_of(z * QUARTER, QUARTER), QUARTER)]
        return remote(mine, mine, a_send.at[k - 1], a_recv.at[k - 1], z_peer(k))

    def stat_copy(k):
        return remote(stat_s, stat_r.at[k - 1], st_send.at[k - 1], st_recv.at[k - 1], z_peer(k))

    for k in range(1, NZ):
        direction_copy(k).start()
        stat_copy(k).start()
    def rs_copy(j, group):
        owner = owner_of(j, group)
        slot = lax.rem(me - owner + NP - 1 + NP, NP)
        return remote(
            rs_s.at[j, group], rs_r.at[slot], rs_send.at[j, group], rs_recv, {"var": z, "samp": owner}
        )

    def project_block(j, stats):
        proj = lax.dot_general(dx[...], xb[j], (((1,), (1,)), ((), ())), preferred_element_type=F32)
        counts = jnp.where(row8 == 0, proj[16:24, :BLK], jnp.where(row8 == 1, proj[16:24, BLK:], stats))
        for group in range(2):
            rs_s[j, group, 0:8, :] = proj[8 * group:8 * group + 8, :BLK]
            rs_s[j, group, 8:16, :] = proj[8 * group:8 * group + 8, BLK:]
            rs_s[j, group, 16:24, :] = counts

            @pl.when(me != owner_of(j, group))
            def _():
                rs_copy(j, group).start()

    def ag_copy(j, group, k):
        return remote(ag_r.at[j, group], ag_r.at[j, group], ag_send, ag_recv.at[j, group], p_peer(k))

    def sq_copy(j, group, k):
        return remote(sq_r.at[j, group], sq_r.at[j, group], sq_send, sq_recv.at[j, group], p_peer(k))

    def owner_part(j):
        first, second = owner_of(j, 0), owner_of(j, 1)

        @pl.when((me == first) | (me == second))
        def _():
            group = (me == second).astype(jnp.int32)
            pltpu.make_async_copy(rs_r, rs_r, rs_recv).wait()
            total = rs_s[j, group] + jnp.sum(rs_r[...], axis=0)
            raw, called = total[0:8], total[8:16]
            frequency = (total[16:17] + 1.0) / (2.0 * total[17:18] + 2.0)
            spread = jnp.sqrt(2.0 * frequency * (1.0 - frequency))
            loading = (raw - 2.0 * frequency * called) / spread
            scaled_a = loading / spread
            scaled_b = 2.0 * frequency * loading / spread
            ag_r[j, group] = jnp.concatenate([scaled_a, -scaled_b], axis=0).astype(BF16)
            each_plane_peer(lambda k: ag_copy(j, group, k).start())
            square = jnp.sum(loading * loading, axis=1, keepdims=True)
            square = jnp.sum(jnp.where(lane8 == row8 + 8 * group, square, 0.0), axis=0, keepdims=True)
            sq_r[j, group] = square + jnp.where(lane8[:1] >= RHS, total[18:19], 0.0)
            each_plane_peer(lambda k: sq_copy(j, group, k).start())

    def back(j):
        halves = []
        for group in range(2):
            @pl.when(me != owner_of(j, group))
            def _():
                ag_copy(j, group, 1).wait_recv()

            halves.append(ag_r[j, group].astype(F32))
        left = jnp.concatenate([half[0:8] for half in halves], axis=0)
        right = jnp.concatenate([half[8:16] for half in halves], axis=0)
        weights = jnp.concatenate([left, right], axis=1).astype(BF16)
        return weights

    def back_product(j, weights):
        g_acc[...] += jnp.dot(weights, xb[j], preferred_element_type=F32)

    each_block(ahead, early, convert_block)
    for k in range(1, NZ):
        stat_copy(k).wait()
    stats = stat_s[...] + stat_r[0] + stat_r[1] + stat_r[2]
    for k in range(1, NZ):
        direction_copy(k).wait()
    each_block(0, early, lambda j: project_block(j, stats))

    def convert_and_project(j):
        convert_block(j)
        project_block(j, stats)

    each_block(early, NBLK, convert_and_project)
    each_block(0, NBLK, owner_part)

    load_dos.wait()

    def one_hot(i, carry):
        first = pl.multiple_of(i * 16, 16)
        hot[pl.ds(first, 16), :] = jnp.where(rows_iota((16, QUARTER)) + first == order[...], 1.0, 0.0).astype(BF16)
        return carry

    lax.fori_loop(0, QUARTER // 16, one_hot, 0)

    def convert_dose(i, carry):
        first = pl.multiple_of(i * 16, 16)
        db[pl.ds(first, 16), :] = dv[pl.ds(first, 16), :].astype(F32).astype(BF16)
        return carry

    lax.fori_loop(0, QUARTER // 16, convert_dose, 0)
    s = sol[...]
    s_high = s.astype(BF16)
    s_low = (s - s_high.astype(F32)).astype(BF16)
    d_low = (d - d_b.astype(F32)).astype(BF16)
    parts = jnp.concatenate([s_high, s_low, d_b, d_low], axis=0)
    picked = jnp.dot(parts, hot[...], preferred_element_type=F32).astype(BF16)
    picked = jnp.concatenate([picked, jnp.ones((RHS, QUARTER), BF16)], axis=0)
    cross = jnp.dot(picked, db[...], preferred_element_type=F32)
    cz_s[0:16, :] = cross[0:16] + cross[16:32]
    cz_s[16:32, :] = cross[32:48] + cross[48:64]
    cz_s[32:40, :] = cross[64:72]
    part = IMPUTED // NZ

    def cz_copy(k):
        peer = lax.rem(z + k, NZ)
        return remote(
            cz_s.at[:, pl.ds(pl.multiple_of(peer * part, part), part)], cz_r.at[k - 1],
            cz_send.at[k - 1], cz_recv.at[k - 1], z_peer(k),
        )

    for k in range(1, NZ):
        cz_copy(k).start()

    each_block(0, NBLK - 1, lambda j: back_product(j, back(j)))

    weights = back(NBLK - 1)

    for j in range(NBLK):
        for group in range(2):
            @pl.when(me != owner_of(j, group))
            def _():
                sq_copy(j, group, 1).wait_recv()

    q_acc[...] = jnp.sum(sq_r[...], axis=(0, 1))

    def q_copy(k):
        return remote(q_acc, q_r.at[k - 1], q_send.at[k - 1], q_recv.at[k - 1], z_peer(k))

    for k in range(1, NZ):
        q_copy(k).start()
    def g_copy(k):
        peer = lax.rem(z + k, NZ)
        return remote(
            g_s.at[:, pl.ds(pl.multiple_of(peer * QUARTER, QUARTER), QUARTER)], g_r.at[k - 1],
            g_send.at[k - 1], g_recv.at[k - 1], z_peer(k),
        )

    for k in (2, 1, 3, 0):
        span = pl.ds(pl.multiple_of(lax.rem(z + k, NZ) * QUARTER, QUARTER), QUARTER)
        g_part = (
            g_acc[:, span] + jnp.dot(weights, xb[NBLK - 1, :, span], preferred_element_type=F32)
        ) * (1.0 / VARIANTS)
        if k:
            g_s[:, span] = g_part.astype(BF16)
            g_copy(k).start()
        else:
            own_g = g_part

    for k in range(1, NZ):
        cz_copy(k).wait()
    own = cz_s[:, pl.ds(pl.multiple_of(z * part, part), part)] + cz_r[0] + cz_r[1] + cz_r[2]
    own = jnp.concatenate([own, jnp.zeros((128 - 40, part), F32)], axis=0)
    cp_s[...] = jnp.transpose(own).reshape(NP, 8, 128)

    def cp_copy(k):
        return remote(cp_s.at[beside(k)], cp_r.at[k - 1], cp_send, cp_recv, p_peer(k))

    each_plane_peer(lambda k: cp_copy(k).start())

    for k in range(1, NZ):
        q_copy(k).wait()
    q = q_acc[...]
    square = (q + q_r[0] + q_r[1] + q_r[2])[:, :RHS]
    res_norm = q[:, RHS:2 * RHS] * (1.0 / (2 * NBLK))
    dir_norm = q[:, 2 * RHS:3 * RHS] * (1.0 / (2 * NBLK))
    curvature = noise[...] * dir_norm + square * (1.0 / VARIANTS)
    step_row = res_norm / (curvature + 1e-6)
    step_col = to_column(step_row)
    s_next = s + step_col * d
    sol_new[...] = s_next
    s_sum = jnp.sum(s_next, axis=1, keepdims=True)
    s_square = jnp.sum(s_next * s_next, axis=1, keepdims=True)
    base = to_column(noise[...]) * d + own_g
    for k in range(1, NZ):
        g_copy(k).wait()
    applied = base + g_r[0].astype(F32) + g_r[1].astype(F32) + g_r[2].astype(F32)
    r_next = r - step_col * applied
    res_new[...] = r_next
    r_square = jnp.sum(r_next * r_next, axis=1, keepdims=True)
    d1_s[...] = spread_columns((r_square, s_sum, s_square))

    def d1_copy(k):
        return remote(d1_s, d1_r.at[k - 1], d1_send.at[k - 1], d1_recv.at[k - 1], z_peer(k))

    for k in range(1, NZ):
        d1_copy(k).start()
    pltpu.make_async_copy(cp_r, cp_r, cp_recv).wait()
    dose = cp_s[me] + jnp.sum(cp_r[...], axis=0)
    for k in range(1, NZ):
        d1_copy(k).wait()
    d2_s[...] = jnp.sum(d1_s[...] + jnp.sum(d1_r[...], axis=0), axis=0, keepdims=True)

    def d2_copy(k):
        return remote(d2_s, d2_r.at[k - 1], d2_send, d2_recv, p_peer(k))

    each_plane_peer(lambda k: d2_copy(k).start())
    dose_freq = (dose[:, 32:33] * (1.0 / 100.0) + 1.0) / (2.0 * SAMPLES + 2.0)
    dose_spread = jnp.sqrt(2.0 * dose_freq * (1.0 - dose_freq))
    cross_sum = dose[:, 0:RHS] + step_row * dose[:, RHS:2 * RHS]
    pltpu.make_async_copy(cp_r, cp_r, cp_send).wait()

    def sent(j, carry):
        for group in range(2):
            @pl.when(me != owner_of(j, group))
            def _():
                rs_copy(j, group).wait_send()

            @pl.when(me == owner_of(j, group))
            def _():
                view = rs_r.at[:, pl.ds(0, 8), :]
                pltpu.make_async_copy(view, view, ag_send).wait()
                pltpu.make_async_copy(d2_r, d2_r, sq_send).wait()

        return carry

    lax.fori_loop(0, NBLK, sent, 0)

    pltpu.make_async_copy(d2_r, d2_r, d2_recv).wait()
    sums = d2_s[...] + jnp.sum(d2_r[...], axis=0)
    beta = to_column(sums[:, 0:RHS] / (res_norm + 1e-6))
    dir_new[...] = r_next + beta * d
    scale = math.sqrt(SAMPLES) * jnp.sqrt(sums[:, 2 * RHS:3 * RHS] * (1.0 / SAMPLES) + 1e-6)
    scores[...] = (cross_sum * (1.0 / 100.0) - 2.0 * dose_freq * sums[:, RHS:2 * RHS]) / (dose_spread * scale)

    pltpu.make_async_copy(d2_r, d2_r, d2_send).wait()


def store_kernel(*refs):
    held, results, sem = refs[:4], refs[4:8], refs[8]
    copies = [pltpu.make_async_copy(held[i], results[i], sem.at[i]) for i in range(4)]
    for copy in copies:
        copy.start()
    for copy in copies:
        copy.wait()


def body(genotypes, called, dosage, sample_order, noise_ratio, solution, residual, direction):
    vmem = pl.BlockSpec(memory_space=pltpu.VMEM)
    hbm = pl.BlockSpec(memory_space=pltpu.HBM)
    dma = pltpu.SemaphoreType.DMA
    small = jax.ShapeDtypeStruct((RHS, QUARTER), F32)
    outs = pl.pallas_call(
        kernel,
        out_shape=(pltpu.VMEM((RHS, QUARTER), F32),) * 3 + (pltpu.VMEM((8, RHS), F32),),
        in_specs=[hbm] * 8,
        out_specs=(vmem,) * 4,
        scratch_shapes=[
            pltpu.VMEM((1, QUARTER), jnp.int32),
            pltpu.VMEM((1, RHS), F32),
            pltpu.VMEM((RHS, QUARTER), F32),
            pltpu.VMEM((RHS, QUARTER), F32),
            pltpu.VMEM((RHS, QUARTER), F32),
            pltpu.VMEM((NBLK, BLK, WIDE), jnp.int32),
            pltpu.VMEM((NBLK, BLK, WIDE), jnp.int32),
            pltpu.VMEM((QUARTER, IMPUTED), jnp.int32),
            pltpu.VMEM((NBLK, 2 * BLK, WIDE), BF16),
            pltpu.VMEM((2 * RHS, WIDE), BF16),
            pltpu.VMEM((QUARTER, IMPUTED), BF16),
            pltpu.VMEM((QUARTER, QUARTER), BF16),
            pltpu.VMEM((8, 128), F32),
            pltpu.VMEM((NZ - 1, 8, 128), F32),
            pltpu.VMEM((NBLK, 2, 24, 128), F32),
            pltpu.VMEM((NP - 1, 24, 128), F32),
            pltpu.VMEM((NBLK, 2, 16, 128), BF16),
            pltpu.VMEM((NBLK, 2, 1, 128), F32),
            pltpu.VMEM((RHS, WIDE), F32),
            pltpu.VMEM((RHS, WIDE), BF16),
            pltpu.VMEM((NZ - 1, RHS, QUARTER), BF16),
            pltpu.VMEM((1, 128), F32),
            pltpu.VMEM((NZ - 1, 1, 128), F32),
            pltpu.VMEM((40, IMPUTED), F32),
            pltpu.VMEM((NZ - 1, 40, IMPUTED // NZ), F32),
            pltpu.VMEM((NP, 8, 128), F32),
            pltpu.VMEM((NP - 1, 8, 128), F32),
            pltpu.VMEM((8, 128), F32),
            pltpu.VMEM((NZ - 1, 8, 128), F32),
            pltpu.VMEM((1, 128), F32),
            pltpu.VMEM((NP - 1, 1, 128), F32),
            dma((5,)),
            dma((2, NBLK + 1)),
            dma((3,)), dma((3,)),
            dma((3,)), dma((3,)),
            dma((NBLK, 2)), dma,
            dma, dma((NBLK, 2)),
            dma, dma((NBLK, 2)),
            dma((3,)), dma((3,)),
            dma((3,)), dma((3,)),
            dma((3,)), dma((3,)),
            dma, dma,
            dma((3,)), dma((3,)),
            dma, dma,
        ],
        compiler_params=pltpu.CompilerParams(
            collective_id=0, has_side_effects=True, vmem_limit_bytes=56 * 1024 * 1024
        ),
        cost_estimate=pl.CostEstimate(flops=400_000_000, bytes_accessed=22_000_000, transcendentals=0),
        name="cg_step",
    )(
        genotypes, called, dosage, sample_order, noise_ratio.reshape(1, RHS),
        solution.T, residual.T, direction.T,
    )
    outs = [pltpu.with_memory_space_constraint(out, pltpu.VMEM) for out in outs]
    sol_new, res_new, dir_new, scores = pl.pallas_call(
        store_kernel,
        out_shape=(small, small, small, jax.ShapeDtypeStruct((8, RHS), F32)),
        in_specs=[vmem] * 4,
        out_specs=(hbm,) * 4,
        scratch_shapes=[dma((4,))],
        cost_estimate=pl.CostEstimate(flops=0, bytes_accessed=300_000, transcendentals=0),
        name="store",
    )(*outs)
    return (sol_new.T, res_new.T, dir_new.T, scores)


def solution(mesh):
    rows = P(("samp", "var"), None)
    return jax.shard_map(
        body,
        mesh=mesh,
        in_specs=(P("var", "samp"), P("var", "samp"), rows, rows, P(), rows, rows, rows),
        out_specs=(rows, rows, rows, P(("var", "samp"), None)),
        check_vma=False,
    )
```

```python
import math

import jax
import jax.numpy as jnp
from jax import lax
from jax.experimental import pallas as pl
from jax.experimental.pallas import tpu as pltpu
from jax.sharding import PartitionSpec as P

VARIANTS = 3072
SAMPLES = 98304
IMPUTED = 1024
RHS = 16
NZ = 4
NP = 32
QUARTER = 768
WIDE = QUARTER * NZ
LOCAL = VARIANTS // NZ
BLK = 128
NBLK = LOCAL // BLK
WINDOW = 3
F32 = jnp.float32
BF16 = jnp.bfloat16
MESH = pl.DeviceIdType.MESH


def owner_of(block, group):
    turn = block + 2
    first = lax.rem(turn, 4) + 4 * (1 - turn // 4)
    second = block + 7
    return 2 * (first + group * (second - first)) + group


def rows_iota(shape):
    return lax.broadcasted_iota(jnp.int32, shape, 0)


def lanes_iota(shape):
    return lax.broadcasted_iota(jnp.int32, shape, 1)


def to_column(row):
    eye = rows_iota((RHS, RHS)) == lanes_iota((RHS, RHS))
    return jnp.sum(jnp.where(eye, jnp.broadcast_to(row, (RHS, RHS)), 0.0), axis=1, keepdims=True)


def spread_columns(columns):
    rows, lanes = rows_iota((RHS, 128)), lanes_iota((RHS, 128))
    total = jnp.zeros((RHS, 128), F32)
    for k, column in enumerate(columns):
        total = jnp.where(lanes == rows + RHS * k, column, total)
    return total[:8] + total[8:]


def kernel(
    gen, cal, dos, order_in, noise_in, sol_in, res_in, dir_in,
    sol_new, res_new, dir_new, scores,
    order, noise, sol, res, dirn, gv, cv, dv, xb, dx, db, hot, stat_s, stat_r, rs_s, rs_r, ag_r, sq_r, g_acc, g_s, g_r,
    q_acc, q_r, cz_s, cz_r, cp_s, cp_r, d1_s, d1_r, d2_s, d2_r,
    in_sem, load_sem, a_send, a_recv, st_send, st_recv, rs_send, rs_recv, ag_send, ag_recv,
    sq_send, sq_recv,
    g_send, g_recv, q_send, q_recv, cz_send, cz_recv, cp_send, cp_recv, d1_send, d1_recv, d2_send, d2_recv,
):
    z = lax.axis_index("var")
    me = lax.axis_index("samp")

    def z_peer(k):
        return {"var": lax.rem(z + k, NZ), "samp": me}

    def beside(k):
        peer = me + k
        return jnp.where(peer >= NP, peer - NP, peer)

    def p_peer(k):
        return {"var": z, "samp": beside(k)}

    def each_block(first, last, work):
        lax.fori_loop(first, last, lambda j, carry: (work(j), carry)[1], 0)

    def each_plane_peer(send):
        for first in (16, 8, 24, 0):
            lax.fori_loop(max(first, 1), first + 8, lambda k, carry: (send(k), carry)[1], 0, unroll=True)

    def remote(src, dst, send, recv, device):
        return pltpu.make_async_remote_copy(
            src_ref=src, dst_ref=dst, send_sem=send, recv_sem=recv, device_id=device, device_id_type=MESH
        )

    def load(j, which):
        source, target = ((gen, gv), (cal, cv))[which]
        return pltpu.make_async_copy(
            source.at[pl.ds(pl.multiple_of(j * BLK, BLK), BLK), :], target.at[j], load_sem.at[which, j]
        )

    load_dos = pltpu.make_async_copy(dos, dv, load_sem.at[0, NBLK])

    smalls = [
        pltpu.make_async_copy(source, target, in_sem.at[i])
        for i, (source, target) in enumerate(
            ((dir_in, dirn), (res_in, res), (sol_in, sol), (noise_in, noise), (order_in, order))
        )
    ]
    for copy in smalls:
        copy.start()
    for j in range(WINDOW):
        load(j, 0).start()
        load(j, 1).start()

    barrier = pltpu.get_barrier_semaphore()
    place = me // 8 + lax.rem(me // 2, 4) + 2 * z
    ahead = jnp.maximum(3 - place // 2, 0)
    early = NBLK - z

    def greet(device):
        pl.semaphore_signal(barrier, inc=1, device_id=device, device_id_type=MESH)

    for k in range(1, NZ):
        greet(z_peer(k))
    each_plane_peer(lambda k: greet(p_peer(k)))
    for copy in smalls:
        copy.wait()

    d = dirn[...]
    r = res[...]
    d_b = d.astype(BF16)
    dx[:RHS, pl.ds(pl.multiple_of(z * QUARTER, QUARTER), QUARTER)] = d_b
    dx[RHS:, :] = jnp.ones((RHS, WIDE), BF16)
    r_col = jnp.sum(r * r, axis=1, keepdims=True)
    d_col = jnp.sum(d * d, axis=1, keepdims=True)
    row8, lane8 = rows_iota((8, 128)), lanes_iota((8, 128))
    pair = jnp.sum(spread_columns((jnp.zeros_like(r_col), r_col, d_col)), axis=0, keepdims=True)
    stat_s[...] = jnp.where(row8 == 2, pair, 0.0)
    g_acc[...] = jnp.zeros((RHS, WIDE), F32)

    def convert_block(j):
        load(j, 0).wait()
        load(j, 1).wait()

        @pl.when(j + WINDOW < NBLK)
        def _():
            load(j + WINDOW, 0).start()
            load(j + WINDOW, 1).start()

        @pl.when(j == NBLK - 1)
        def _():
            load_dos.start()

        def convert(i, carry):
            first = pl.multiple_of(i * 16, 16)
            called = cv[j, pl.ds(first, 16), :].astype(F32).astype(BF16)
            codes = gv[j, pl.ds(first, 16), :].astype(F32).astype(BF16)
            xb[j, pl.ds(first, 16), :] = codes * called
            xb[j, pl.ds(pl.multiple_of(first + BLK, 16), 16), :] = called
            return carry

        lax.fori_loop(0, BLK // 16, convert, 0)

    each_block(0, ahead, convert_block)
    pl.semaphore_wait(barrier, NP - 1 + NZ - 1)

    def direction_copy(k):
        mine = dx.at[pl.ds(0, RHS), pl.ds(pl.multiple_of(z * QUARTER, QUARTER), QUARTER)]
        return remote(mine, mine, a_send.at[k - 1], a_recv.at[k - 1], z_peer(k))

    def stat_copy(k):
        return remote(stat_s, stat_r.at[k - 1], st_send.at[k - 1], st_recv.at[k - 1], z_peer(k))

    for k in range(1, NZ):
        direction_copy(k).start()
        stat_copy(k).start()
    def rs_copy(j, group):
        owner = owner_of(j, group)
        slot = lax.rem(me - owner + NP - 1 + NP, NP)
        return remote(
            rs_s.at[j, group], rs_r.at[slot], rs_send.at[j, group], rs_recv, {"var": z, "samp": owner}
        )

    def project_block(j, stats):
        proj = lax.dot_general(dx[...], xb[j], (((1,), (1,)), ((), ())), preferred_element_type=F32)
        counts = jnp.where(row8 == 0, proj[16:24, :BLK], jnp.where(row8 == 1, proj[16:24, BLK:], stats))
        for group in range(2):
            rs_s[j, group, 0:8, :] = proj[8 * group:8 * group + 8, :BLK]
            rs_s[j, group, 8:16, :] = proj[8 * group:8 * group + 8, BLK:]
            rs_s[j, group, 16:24, :] = counts

            @pl.when(me != owner_of(j, group))
            def _():
                rs_copy(j, group).start()

    def ag_copy(j, group, k):
        return remote(ag_r.at[j, group], ag_r.at[j, group], ag_send, ag_recv.at[j, group], p_peer(k))

    def sq_copy(j, group, k):
        return remote(sq_r.at[j, group], sq_r.at[j, group], sq_send, sq_recv.at[j, group], p_peer(k))

    def owner_part(j):
        first, second = owner_of(j, 0), owner_of(j, 1)

        @pl.when((me == first) | (me == second))
        def _():
            group = (me == second).astype(jnp.int32)
            pltpu.make_async_copy(rs_r, rs_r, rs_recv).wait()
            total = rs_s[j, group] + jnp.sum(rs_r[...], axis=0)
            raw, called = total[0:8], total[8:16]
            frequency = (total[16:17] + 1.0) / (2.0 * total[17:18] + 2.0)
            spread = jnp.sqrt(2.0 * frequency * (1.0 - frequency))
            loading = (raw - 2.0 * frequency * called) / spread
            scaled_a = loading / spread
            scaled_b = 2.0 * frequency * loading / spread
            ag_r[j, group] = jnp.concatenate([scaled_a, -scaled_b], axis=0).astype(BF16)
            each_plane_peer(lambda k: ag_copy(j, group, k).start())
            square = jnp.sum(loading * loading, axis=1, keepdims=True)
            square = jnp.sum(jnp.where(lane8 == row8 + 8 * group, square, 0.0), axis=0, keepdims=True)
            sq_r[j, group] = square + jnp.where(lane8[:1] >= RHS, total[18:19], 0.0)
            each_plane_peer(lambda k: sq_copy(j, group, k).start())

    def back(j):
        halves = []
        for group in range(2):
            @pl.when(me != owner_of(j, group))
            def _():
                ag_copy(j, group, 1).wait_recv()

            halves.append(ag_r[j, group].astype(F32))
        left = jnp.concatenate([half[0:8] for half in halves], axis=0)
        right = jnp.concatenate([half[8:16] for half in halves], axis=0)
        weights = jnp.concatenate([left, right], axis=1).astype(BF16)
        return weights

    def back_product(j, weights):
        g_acc[...] += jnp.dot(weights, xb[j], preferred_element_type=F32)

    each_block(ahead, early, convert_block)
    for k in range(1, NZ):
        stat_copy(k).wait()
    stats = stat_s[...] + stat_r[0] + stat_r[1] + stat_r[2]
    for k in range(1, NZ):
        direction_copy(k).wait()

    def convert_and_project(j):
        @pl.when(j >= early)
        def _():
            convert_block(j)

        project_block(j, stats)

    each_block(0, NBLK, convert_and_project)
    each_block(0, NBLK, owner_part)

    load_dos.wait()

    def one_hot(i, carry):
        first = pl.multiple_of(i * 16, 16)
        hot[pl.ds(first, 16), :] = jnp.where(rows_iota((16, QUARTER)) + first == order[...], 1.0, 0.0).astype(BF16)
        return carry

    lax.fori_loop(0, QUARTER // 16, one_hot, 0)

    def convert_dose(i, carry):
        first = pl.multiple_of(i * 16, 16)
        db[pl.ds(first, 16), :] = dv[pl.ds(first, 16), :].astype(F32).astype(BF16)
        return carry

    lax.fori_loop(0, QUARTER // 16, convert_dose, 0)
    s = sol[...]
    s_high = s.astype(BF16)
    s_low = (s - s_high.astype(F32)).astype(BF16)
    d_low = (d - d_b.astype(F32)).astype(BF16)
    parts = jnp.concatenate([s_high, s_low, d_b, d_low], axis=0)
    picked = jnp.dot(parts, hot[...], preferred_element_type=F32).astype(BF16)
    picked = jnp.concatenate([picked, jnp.ones((RHS, QUARTER), BF16)], axis=0)
    cross = jnp.dot(picked, db[...], preferred_element_type=F32)
    cz_s[0:16, :] = cross[0:16] + cross[16:32]
    cz_s[16:32, :] = cross[32:48] + cross[48:64]
    cz_s[32:40, :] = cross[64:72]
    part = IMPUTED // NZ

    def cz_copy(k):
        peer = lax.rem(z + k, NZ)
        return remote(
            cz_s.at[:, pl.ds(pl.multiple_of(peer * part, part), part)], cz_r.at[k - 1],
            cz_send.at[k - 1], cz_recv.at[k - 1], z_peer(k),
        )

    for k in range(1, NZ):
        cz_copy(k).start()

    each_block(0, NBLK - 1, lambda j: back_product(j, back(j)))

    weights = back(NBLK - 1)

    for j in range(NBLK):
        for group in range(2):
            @pl.when(me != owner_of(j, group))
            def _():
                sq_copy(j, group, 1).wait_recv()

    q_acc[...] = jnp.sum(sq_r[...], axis=(0, 1))

    def q_copy(k):
        return remote(q_acc, q_r.at[k - 1], q_send.at[k - 1], q_recv.at[k - 1], z_peer(k))

    for k in range(1, NZ):
        q_copy(k).start()
    def g_copy(k):
        peer = lax.rem(z + k, NZ)
        return remote(
            g_s.at[:, pl.ds(pl.multiple_of(peer * QUARTER, QUARTER), QUARTER)], g_r.at[k - 1],
            g_send.at[k - 1], g_recv.at[k - 1], z_peer(k),
        )

    for k in (2, 1, 3, 0):
        span = pl.ds(pl.multiple_of(lax.rem(z + k, NZ) * QUARTER, QUARTER), QUARTER)
        g_part = (
            g_acc[:, span] + jnp.dot(weights, xb[NBLK - 1, :, span], preferred_element_type=F32)
        ) * (1.0 / VARIANTS)
        if k:
            g_s[:, span] = g_part.astype(BF16)
            g_copy(k).start()
        else:
            own_g = g_part

    for k in range(1, NZ):
        cz_copy(k).wait()
    own = cz_s[:, pl.ds(pl.multiple_of(z * part, part), part)] + cz_r[0] + cz_r[1] + cz_r[2]
    own = jnp.concatenate([own, jnp.zeros((128 - 40, part), F32)], axis=0)
    cp_s[...] = jnp.transpose(own).reshape(NP, 8, 128)

    def cp_copy(k):
        return remote(cp_s.at[beside(k)], cp_r.at[k - 1], cp_send, cp_recv, p_peer(k))

    each_plane_peer(lambda k: cp_copy(k).start())

    for k in range(1, NZ):
        q_copy(k).wait()
    q = q_acc[...]
    square = (q + q_r[0] + q_r[1] + q_r[2])[:, :RHS]
    res_norm = q[:, RHS:2 * RHS] * (1.0 / (2 * NBLK))
    dir_norm = q[:, 2 * RHS:3 * RHS] * (1.0 / (2 * NBLK))
    curvature = noise[...] * dir_norm + square * (1.0 / VARIANTS)
    step_row = res_norm / (curvature + 1e-6)
    step_col = to_column(step_row)
    s_next = s + step_col * d
    sol_new[...] = s_next
    s_sum = jnp.sum(s_next, axis=1, keepdims=True)
    s_square = jnp.sum(s_next * s_next, axis=1, keepdims=True)
    base = to_column(noise[...]) * d + own_g
    for k in range(1, NZ):
        g_copy(k).wait()
    applied = base + g_r[0].astype(F32) + g_r[1].astype(F32) + g_r[2].astype(F32)
    r_next = r - step_col * applied
    res_new[...] = r_next
    r_square = jnp.sum(r_next * r_next, axis=1, keepdims=True)
    d1_s[...] = spread_columns((r_square, s_sum, s_square))

    def d1_copy(k):
        return remote(d1_s, d1_r.at[k - 1], d1_send.at[k - 1], d1_recv.at[k - 1], z_peer(k))

    for k in range(1, NZ):
        d1_copy(k).start()
    pltpu.make_async_copy(cp_r, cp_r, cp_recv).wait()
    dose = cp_s[me] + jnp.sum(cp_r[...], axis=0)
    for k in range(1, NZ):
        d1_copy(k).wait()
    d2_s[...] = jnp.sum(d1_s[...] + jnp.sum(d1_r[...], axis=0), axis=0, keepdims=True)

    def d2_copy(k):
        return remote(d2_s, d2_r.at[k - 1], d2_send, d2_recv, p_peer(k))

    each_plane_peer(lambda k: d2_copy(k).start())
    dose_freq = (dose[:, 32:33] * (1.0 / 100.0) + 1.0) / (2.0 * SAMPLES + 2.0)
    dose_spread = jnp.sqrt(2.0 * dose_freq * (1.0 - dose_freq))
    cross_sum = dose[:, 0:RHS] + step_row * dose[:, RHS:2 * RHS]
    pltpu.make_async_copy(cp_r, cp_r, cp_send).wait()

    def sent(j, carry):
        for group in range(2):
            @pl.when(me != owner_of(j, group))
            def _():
                rs_copy(j, group).wait_send()

            @pl.when(me == owner_of(j, group))
            def _():
                view = rs_r.at[:, pl.ds(0, 8), :]
                pltpu.make_async_copy(view, view, ag_send).wait()
                pltpu.make_async_copy(d2_r, d2_r, sq_send).wait()

        return carry

    lax.fori_loop(0, NBLK, sent, 0)

    pltpu.make_async_copy(d2_r, d2_r, d2_recv).wait()
    sums = d2_s[...] + jnp.sum(d2_r[...], axis=0)
    beta = to_column(sums[:, 0:RHS] / (res_norm + 1e-6))
    dir_new[...] = r_next + beta * d
    scale = math.sqrt(SAMPLES) * jnp.sqrt(sums[:, 2 * RHS:3 * RHS] * (1.0 / SAMPLES) + 1e-6)
    scores[...] = (cross_sum * (1.0 / 100.0) - 2.0 * dose_freq * sums[:, RHS:2 * RHS]) / (dose_spread * scale)

    pltpu.make_async_copy(d2_r, d2_r, d2_send).wait()


def store_kernel(*refs):
    held, results, sem = refs[:4], refs[4:8], refs[8]
    copies = [pltpu.make_async_copy(held[i], results[i], sem.at[i]) for i in range(4)]
    for copy in copies:
        copy.start()
    for copy in copies:
        copy.wait()


def body(genotypes, called, dosage, sample_order, noise_ratio, solution, residual, direction):
    vmem = pl.BlockSpec(memory_space=pltpu.VMEM)
    hbm = pl.BlockSpec(memory_space=pltpu.HBM)
    dma = pltpu.SemaphoreType.DMA
    small = jax.ShapeDtypeStruct((RHS, QUARTER), F32)
    outs = pl.pallas_call(
        kernel,
        out_shape=(pltpu.VMEM((RHS, QUARTER), F32),) * 3 + (pltpu.VMEM((8, RHS), F32),),
        in_specs=[hbm] * 8,
        out_specs=(vmem,) * 4,
        scratch_shapes=[
            pltpu.VMEM((1, QUARTER), jnp.int32),
            pltpu.VMEM((1, RHS), F32),
            pltpu.VMEM((RHS, QUARTER), F32),
            pltpu.VMEM((RHS, QUARTER), F32),
            pltpu.VMEM((RHS, QUARTER), F32),
            pltpu.VMEM((NBLK, BLK, WIDE), jnp.int32),
            pltpu.VMEM((NBLK, BLK, WIDE), jnp.int32),
            pltpu.VMEM((QUARTER, IMPUTED), jnp.int32),
            pltpu.VMEM((NBLK, 2 * BLK, WIDE), BF16),
            pltpu.VMEM((2 * RHS, WIDE), BF16),
            pltpu.VMEM((QUARTER, IMPUTED), BF16),
            pltpu.VMEM((QUARTER, QUARTER), BF16),
            pltpu.VMEM((8, 128), F32),
            pltpu.VMEM((NZ - 1, 8, 128), F32),
            pltpu.VMEM((NBLK, 2, 24, 128), F32),
            pltpu.VMEM((NP - 1, 24, 128), F32),
            pltpu.VMEM((NBLK, 2, 16, 128), BF16),
            pltpu.VMEM((NBLK, 2, 1, 128), F32),
            pltpu.VMEM((RHS, WIDE), F32),
            pltpu.VMEM((RHS, WIDE), BF16),
            pltpu.VMEM((NZ - 1, RHS, QUARTER), BF16),
            pltpu.VMEM((1, 128), F32),
            pltpu.VMEM((NZ - 1, 1, 128), F32),
            pltpu.VMEM((40, IMPUTED), F32),
            pltpu.VMEM((NZ - 1, 40, IMPUTED // NZ), F32),
            pltpu.VMEM((NP, 8, 128), F32),
            pltpu.VMEM((NP - 1, 8, 128), F32),
            pltpu.VMEM((8, 128), F32),
            pltpu.VMEM((NZ - 1, 8, 128), F32),
            pltpu.VMEM((1, 128), F32),
            pltpu.VMEM((NP - 1, 1, 128), F32),
            dma((5,)),
            dma((2, NBLK + 1)),
            dma((3,)), dma((3,)),
            dma((3,)), dma((3,)),
            dma((NBLK, 2)), dma,
            dma, dma((NBLK, 2)),
            dma, dma((NBLK, 2)),
            dma((3,)), dma((3,)),
            dma((3,)), dma((3,)),
            dma((3,)), dma((3,)),
            dma, dma,
            dma((3,)), dma((3,)),
            dma, dma,
        ],
        compiler_params=pltpu.CompilerParams(
            collective_id=0, has_side_effects=True, vmem_limit_bytes=56 * 1024 * 1024
        ),
        cost_estimate=pl.CostEstimate(flops=400_000_000, bytes_accessed=22_000_000, transcendentals=0),
        name="cg_step",
    )(
        genotypes, called, dosage, sample_order, noise_ratio.reshape(1, RHS),
        solution.T, residual.T, direction.T,
    )
    outs = [pltpu.with_memory_space_constraint(out, pltpu.VMEM) for out in outs]
    sol_new, res_new, dir_new, scores = pl.pallas_call(
        store_kernel,
        out_shape=(small, small, small, jax.ShapeDtypeStruct((8, RHS), F32)),
        in_specs=[vmem] * 4,
        out_specs=(hbm,) * 4,
        scratch_shapes=[dma((4,))],
        cost_estimate=pl.CostEstimate(flops=0, bytes_accessed=300_000, transcendentals=0),
        name="store",
    )(*outs)
    return (sol_new.T, res_new.T, dir_new.T, scores)


def solution(mesh):
    rows = P(("samp", "var"), None)
    return jax.shard_map(
        body,
        mesh=mesh,
        in_specs=(P("var", "samp"), P("var", "samp"), rows, rows, P(), rows, rows, rows),
        out_specs=(rows, rows, rows, P(("var", "samp"), None)),
        check_vma=False,
    )
```
